128 devices in a mesh: grp: 4 (over y), dev: 32 (over z, x, core).
Axes of the slice: x: 4, y: 4, z: 4, core: 2. Of those that a mesh axis runs over, the one named last changes fastest.
Arguments:
- face_owner: int32 [524288, 1], P(('grp', 'dev')), may hold values from 0 to 127; in each aligned block of 4096 rows (0 to 4095, 4096 to 8191, ...) at most 64 rows name the same one
- face_element: int32 [524288], P(('grp', 'dev')), may hold values from 0 to 16383
- element_state: bfloat16 [110, 524288], P(None, ('grp', 'dev')), may hold values from -6 to 6
- lift: bfloat16 [30, 110], replicated, may hold values from -0.5 to 0.5
- face_scale: float32 [524288], P(('grp', 'dev')), may hold values from 0.5 to 2
- transfer: float32 [4, 10], replicated, may hold values from 0.05 to 0.5
- stiffness_ref: float32 [12, 12], replicated, may hold values from -0.18 to 5, as said below
- element_scale: float32 [256, 8192], P('grp', 'dev'), may hold values from 1 to 1.1
- displacement_prev: float32 [4, 3, 256, 8192], P(None, None, 'grp', 'dev'), may hold values from -6 to 6
Outputs:
- shell_displacement: float32 [4, 3, 256, 8192], P(None, None, 'grp', 'dev')
- face_displacement: float32 [3, 10, 524288], P(None, None, ('grp', 'dev'))
The draws below stay inside these ranges and needn't reach their ends.
Inputs may be any that keep to these rules, and one draw needn't show every extreme that they name: `face_owner`: among the 4096 faces of one device (aligned blocks), at most 64 name the same owner, and in every draw some device has exactly 64 faces on one owner. `stiffness_ref`: every diagonal entry is 5 and the off-diagonal entries of each row have absolute values summing to at most 2.
All inputs are finite; a program needn't handle non-finite values.
Results may differ from the reference program's by a relative error of at most 0.0003.
Values sent between devices are 32-bit elements; how exact they have to be, the bound alone decides.
No kernel may reach another device: no remote copies, remote signals or barrier semaphores. Data moves between devices by JAX's collectives and lax.ppermute only.
A program may use at most 128 MiB of HBM per device.

```python
import math
import jax
import jax.numpy as jnp
import numpy as np
from jax import lax

NODES_F = 10
STATE = 110
SWEEPS = 8
FACES_DEV = 4096
SX = 64
SY = 256
CAP = 64
FACES = 524288
N_GRP = 4
N_DEV = 32
DEVICES = 128


def draw_stiffness_ref(key, part):
    key_one = jax.random.fold_in(jax.random.fold_in(key, 7), 0)
    spread = jax.random.uniform(key_one, (12, 12), jnp.float32, -0.18, 0.18)
    identity = jnp.eye(12, dtype=jnp.float32)
    return spread * (1.0 - identity) + 5.0 * identity


def set_ends(result, rng, low, high):
    shape = result.shape
    place = [jax.random.randint(jax.random.fold_in(rng, axis), (), 0, shape[axis]) for axis in range(len(shape))]
    result = result.at[tuple(place)].set(low)
    longest = shape.index(max(shape))
    place[longest] = (place[longest] + 1) % shape[longest]
    return result.at[tuple(place)].set(high)


def block_scale(rng, dims, shards, low, top_value):
    def one(position, blocks):
        draws = jax.random.uniform(jax.random.fold_in(jax.random.fold_in(rng, 6), position), (blocks,), jnp.float32, low / len(shards), top_value / len(shards))
        return jnp.repeat(jnp.exp(draws), dims[position] // blocks).reshape((-1,) + (1,) * (len(dims) - position - 1))

    factor_of = one(*shards[0])
    for cut in shards[1:]:
        factor_of = factor_of * one(*cut)
    return factor_of


def assign_block(rng, own, number, rows, number_of, top, reach, skew):
    sequence = jax.random.permutation(rng, number_of)
    packed, ordinary = shares(number_of, rows * top, reach, skew, True), shares(number_of, rows * top, reach, skew, False)
    places = jnp.arange(number_of)

    def named(sizes, turn):
        used = int((sizes > 0).sum())
        fixed = max(1, used // 4)
        moved = fixed + (places - fixed + turn * (used - fixed)) % max(1, number_of - fixed)
        return jnp.zeros((number_of,), jnp.int32).at[sequence[jnp.where(places < fixed, places, moved)]].set(jnp.asarray(sizes, jnp.int32))

    sizes = jnp.where(number % 4 == 0, named(packed, number // 4), named(ordinary, number - number // 4 - 1))
    mixed = jax.random.permutation(jax.random.fold_in(own, 3), number_of)
    giver, receiver = mixed[0:number_of // 2 * 2:2], mixed[1:number_of // 2 * 2:2]
    slack = jnp.minimum(sizes[giver] - 1, reach - sizes[receiver]) // 2
    slack = jnp.where((giver == sequence[0]) | (receiver == sequence[0]) | (sizes[receiver] == 0), 0, jnp.maximum(slack, 0))
    moved = jax.random.randint(jax.random.fold_in(own, 4), (number_of // 2,), 0, 1 << 20) % (slack + 1)
    sizes = sizes.at[giver].add(-moved).at[receiver].add(moved)
    labels = jnp.searchsorted(jnp.cumsum(sizes), jnp.arange(rows * top), side="right").astype(jnp.int32)
    listing = labels.reshape(top, rows).T
    listing = listing[jax.random.permutation(jax.random.fold_in(own, 1), rows)]
    turn = jax.random.randint(jax.random.fold_in(own, 2), (rows, 1), 0, top)
    return jnp.take_along_axis(listing, (jnp.arange(top)[None, :] + turn) % top, axis=1)


def shares(number_of, total, limit, skew, full):
    weights = [(1 << 20) // math.isqrt(rank ** skew) + 1 for rank in range(1, number_of + 1)]
    largest = limit if full else min(limit, max(-(-total // number_of), total * weights[0] // sum(weights)))
    least = 1 if total - largest >= number_of - 1 else 0
    given, spare = [largest] + [least] * (number_of - 1), total - largest - least * (number_of - 1)
    while spare > 0:
        free = [i for i in range(1, number_of) if given[i] < largest] or [i for i in range(1, number_of) if given[i] < limit]
        mass, budget = sum([weights[i] for i in free]), spare
        for i in free:
            extra = min(limit - given[i], max(1, budget * weights[i] // mass), spare)
            given[i] = given[i] + extra
            spare = spare - extra
    return np.array(given)


def normal_values(rng, shape, width, most, cuts=(), kind=jnp.bfloat16):
    entries = width * jax.random.normal(rng, shape, jnp.float32)
    if cuts:
        entries = entries * block_scale(rng, shape, cuts, -0.22, 0.18)
    return jnp.clip(entries, -most, most).astype(kind)


def setup_inputs(seed: int = 0) -> dict:
    key_of = jax.random.split(jax.random.key(seed), 10)
    face_owner_keys = jax.random.split(jax.random.fold_in(key_of[0], 1), FACES // FACES_DEV)
    face_owner_turns = jax.random.permutation(jax.random.fold_in(key_of[0], 3), FACES // FACES_DEV)
    face_owner = jax.vmap(lambda own, number: assign_block(jax.random.fold_in(key_of[0], 2), own, number, FACES_DEV, DEVICES, 1, CAP, 1))(face_owner_keys, face_owner_turns).reshape((FACES, 1))
    face_element = set_ends(jax.random.randint(key_of[1], (FACES,), 0, SX * SY), jax.random.fold_in(key_of[1], 1), 0, (SX * SY) - 1).astype(jnp.int32)
    element_state = normal_values(key_of[2], (STATE, FACES), 1.0, 6.0, ((1, 128),))
    lift = normal_values(key_of[3], (3 * NODES_F, STATE), STATE ** -0.5, 0.5)
    face_scale = jnp.clip(jnp.exp(math.log(2.0) - 1.3862944 * jax.random.uniform(key_of[4], (FACES,), jnp.float32) ** block_scale(key_of[4], (FACES,), ((0, 128),), -0.2, 0.2)), 0.5, 2.0)
    transfer = jnp.clip(jax.random.uniform(key_of[5], (4, NODES_F), jnp.float32, 0.05, 0.5), 0.05, 0.5)
    stiffness_ref = draw_stiffness_ref(jax.random.fold_in(key_of[9], 71), 0)
    element_scale = jnp.clip(jnp.exp(math.log(1.1) - 0.095310201 * jax.random.uniform(key_of[7], (SX * N_GRP, SY * N_DEV), jnp.float32) ** block_scale(key_of[7], (SX * N_GRP, SY * N_DEV), ((0, 4), (1, 32)), -0.2, 0.2)), 1.0, 1.1)
    displacement_prev = normal_values(key_of[8], (4, 3, SX * N_GRP, SY * N_DEV), 1.0, 6.0, ((2, 4), (3, 32)), jnp.float32)
    return dict(face_owner=face_owner, face_element=face_element, element_state=element_state, lift=lift, face_scale=face_scale, transfer=transfer, stiffness_ref=stiffness_ref, element_scale=element_scale, displacement_prev=displacement_prev)


coupling_weight = 2.2
highest = lax.Precision.HIGHEST


def invert_block(stiffness_ref):
    identity = jnp.eye(12, dtype=jnp.float32)
    approx = identity / 5.0
    for turn_index in range(8):
        product = jnp.dot(stiffness_ref, approx, precision=highest, preferred_element_type=jnp.float32)
        approx = jnp.dot(approx, 2.0 * identity - product, precision=highest, preferred_element_type=jnp.float32)
    return approx


def couple(padded):
    east_side = padded[:, :, 1:-1, 2:]
    west_side = padded[:, :, 1:-1, :-2]
    north_side = padded[:, :, 2:, 1:-1]
    south_side = padded[:, :, :-2, 1:-1]
    return jnp.stack([west_side[1] + south_side[2], east_side[0] + south_side[3],
                      west_side[3] + north_side[0], east_side[2] + north_side[1]])


def jacobi_sweep(displacement, padded, shell_load, block_inverse, element_scale):
    right_side = shell_load + coupling_weight * couple(padded)
    solved = jnp.dot(block_inverse, right_side.reshape(12, -1), precision=highest, preferred_element_type=jnp.float32)
    return solved.reshape(displacement.shape) / element_scale


def reference(face_owner, face_element, element_state, lift, face_scale, transfer, stiffness_ref, element_scale, displacement_prev):
    traces = jnp.dot(lift, element_state, preferred_element_type=jnp.float32) * face_scale[None, :]
    traction = traces.reshape(3, NODES_F, -1)
    face_load = jnp.einsum("nk,ckf->ncf", transfer, traction, precision=highest).reshape(12, -1)
    owners = face_owner[:, 0]
    grid_width = SY * N_DEV
    grid_row = (owners // N_DEV) * SX + face_element // SY
    grid_col = (owners % N_DEV) * SY + face_element % SY
    target = (grid_row * grid_width + grid_col).astype(jnp.int32)
    shell_load = jnp.zeros((12, SX * N_GRP * grid_width), jnp.float32).at[:, target].add(face_load)
    shell_load = shell_load.reshape(4, 3, SX * N_GRP, grid_width)
    block_inverse = invert_block(stiffness_ref)
    displacement = displacement_prev
    for turn_index in range(SWEEPS):
        padded = jnp.pad(displacement, ((0, 0), (0, 0), (1, 1), (1, 1)))
        displacement = jacobi_sweep(displacement, padded, shell_load, block_inverse, element_scale)
    node_disp = displacement.reshape(12, -1)[:, target].reshape(4, 3, -1)
    face_displacement = jnp.einsum("nk,ncf->ckf", transfer, node_disp, precision=highest)
    return displacement, face_displacement
```

```python
import functools

import jax
import jax.numpy as jnp
from jax import lax
from jax.experimental import pallas as pl
from jax.experimental.pallas import tpu as pltpu
from jax.sharding import PartitionSpec as P

SWEEPS = 8
WEIGHT = 2.2
HIGHEST = lax.Precision.HIGHEST
F32 = jnp.float32
BF16 = jnp.bfloat16
I32 = jnp.int32

OWNERS = 128
CAP = 64
COLS = 256
ROWS = 64
PAD_R = 80
PAD_C = 384
FACES = 4096
CHUNK = 256
NT = (((1,), (1,)), ((), ()))


def iota(shape, dim):
    return lax.broadcasted_iota(I32, shape, dim)


def dot(a, b):
    return jnp.dot(a, b, preferred_element_type=F32)


def dot_nt(a, b):
    return lax.dot_general(a, b, NT, preferred_element_type=F32)


def exact(a, b):
    return jnp.dot(a, b, precision=HIGHEST, preferred_element_type=F32)


def one_hot(flag):
    return flag.astype(F32).astype(BF16)


def split(x):
    high = x.astype(BF16)
    return high, (x - high.astype(F32)).astype(BF16)


def face_kernel(owner_ref, elem_ref, state_ref, scale_ref, lift_ref, transfer_ref, msg_ref, rank_ref, x_ref, acc_ref):
    by_node = exact((iota((12, 4), 0) // 3 == iota((12, 4), 1)).astype(F32), transfer_ref[...])
    spread = exact(by_node, (iota((10, 30), 1) % 10 == iota((10, 30), 0)).astype(F32))
    spread = jnp.where(iota((12, 30), 0) % 3 == iota((12, 30), 1) // 10, spread, 0.0)
    weights = exact(spread, lift_ref[...].astype(F32))
    high, low = split(weights)
    x_ref[...] = jnp.zeros_like(x_ref)
    acc_ref[...] = jnp.zeros_like(acc_ref)
    before = iota((CHUNK, 2 * CHUNK), 0)
    upper = iota((CHUNK, 2 * CHUNK), 1)
    upper = one_hot((before < upper) | (upper >= CHUNK))

    def body(i, base):
        part = pl.ds(pl.multiple_of(i * CHUNK, CHUNK), CHUNK)
        hot = (iota((OWNERS, CHUNK), 0) == owner_ref[:, part]).astype(F32)
        hot16 = hot.astype(BF16)
        counts = dot(hot16, upper)
        rank = jnp.sum(hot * (counts[:, :CHUNK] + base), axis=0, keepdims=True)
        rank_ref[:, part] = rank
        place = one_hot(iota((CAP, CHUNK), 0).astype(F32) == rank)
        state = state_ref[:, part]
        load = (dot(high, state) + dot(low, state)) * scale_ref[:, part]
        marker = (elem_ref[:, part] + 1).astype(F32)
        for c in range(13):
            row = load[c:c + 1] if c < 12 else marker
            top, rest = split(jnp.broadcast_to(row, (16, CHUNK)))
            for k in range(CAP // 16):
                at = c * CAP + 16 * k
                x_ref[at:at + 16, :CHUNK] = place[16 * k:16 * k + 16] * top
                x_ref[at:at + 16, CHUNK:] = place[16 * k:16 * k + 16] * rest
        acc_ref[...] += dot_nt(jnp.concatenate([hot16, hot16], axis=1), x_ref[...])
        return base + counts[:, CHUNK:]

    lax.fori_loop(0, FACES // CHUNK, body, jnp.zeros((OWNERS, CHUNK), F32))
    for j in range(7):
        msg_ref[:, j, :] = acc_ref[:, 128 * j:128 * j + 128]
    msg_ref[:, 7, :] = jnp.zeros((OWNERS, 128), F32)


def pair_up(a, b):
    first = iota((8, 128), 1) < 64
    even = jnp.where(first, a, pltpu.roll(b, 64, 1))
    odd = jnp.where(first, pltpu.roll(a, 64, 1), b)
    return even, odd


def element_of(marker):
    element = marker.astype(I32) - 1
    return element >> 8, element & 255


def edge_sends(comps, west_ref, east_ref):
    lane = iota((ROWS, 128), 1)
    west = jnp.zeros((ROWS, 128), F32)
    east = jnp.zeros((ROWS, 128), F32)
    for i, comp in enumerate(comps):
        here = lane // 8 == i
        low = comp(0)
        high = comp(128)
        west = jnp.where(here, pltpu.roll(low, 8 * i, 1) if i else low, west)
        east = jnp.where(here, pltpu.roll(high, (8 * i + 8) % 128, 1), east)
    west_ref[...] = west
    east_ref[...] = east


PAIRS = 4


def scatter_kernel(msg_ref, load_ref, west_ref, east_ref, a_ref, col_ref, acc_ref):
    acc_ref[...] = jnp.zeros_like(acc_ref)

    def body(i, carry):
        for q in range(PAIRS):
            even, odd = pair_up(msg_ref[2 * (i * PAIRS + q)], msg_ref[2 * (i * PAIRS + q) + 1])
            row, col = element_of(even[6:7])
            row_hot = one_hot(iota((ROWS, 128), 0) == row)
            col_hot = one_hot(iota((COLS, 128), 0) == col)
            lanes = 256 * q
            col_ref[:, lanes:lanes + 128] = col_hot
            col_ref[:, lanes + 128:lanes + 256] = col_hot
            for c in range(12):
                value = (odd if c % 2 else even)[c // 2:c // 2 + 1] * (1.0 / WEIGHT)
                top, rest = split(jnp.broadcast_to(value, (16, 128)))
                for k in range(ROWS // 16):
                    at = c * ROWS + 16 * k
                    a_ref[at:at + 16, lanes:lanes + 128] = row_hot[16 * k:16 * k + 16] * top
                    a_ref[at:at + 16, lanes + 128:lanes + 256] = row_hot[16 * k:16 * k + 16] * rest
        acc_ref[...] += dot_nt(a_ref[...], col_ref[...])
        return carry

    lax.fori_loop(0, OWNERS // 2 // PAIRS, body, 0)
    for c in range(12):
        load_ref[c] = acc_ref[c * ROWS:(c + 1) * ROWS]
    edge_sends(
        [(lambda lane, c=c: acc_ref[c * ROWS:(c + 1) * ROWS, lane:lane + 128]) for c in range(12)],
        west_ref, east_ref,
    )


def edge_kernel(prev_ref, scale_ref, stiff_ref, west_ref, east_ref, mat_ref):
    comps = [(lambda lane, c=c: prev_ref[c, :, lane:lane + 128]) for c in range(12)]
    comps.append(lambda lane: scale_ref[:, lane:lane + 128])
    edge_sends(comps, west_ref, east_ref)
    eye = (iota((12, 12), 0) == iota((12, 12), 1)).astype(F32)
    approx = eye / 5.0
    rest = eye - exact(stiff_ref[...], approx)
    for turn in range(8):
        approx = approx + exact(approx, rest)
        if turn < 7:
            rest = exact(rest, rest)
    tall = (iota((192, 12), 0) // 16 == iota((192, 12), 1)).astype(F32)
    wide = (iota((12, 192), 1) // 16 == iota((12, 192), 0)).astype(F32)
    big = exact(exact(tall, approx * WEIGHT), wide)
    big = jnp.where(iota((192, 192), 0) % 16 == iota((192, 192), 1) % 16, big, 0.0)
    high, low = split(big)
    mat_ref[0] = high
    mat_ref[1] = low


def rows_kernel(count, refs):
    cores, (from_east_ref, from_west_ref, side_ref, north_ref, south_ref) = refs[:count], refs[count:]
    at = 0
    lane = iota((ROWS, 128), 1)
    dev = lax.axis_index("dev")
    from_east = jnp.where(dev < lax.axis_size("dev") - 1, from_east_ref[...], 0.0)
    from_west = jnp.where(dev > 0, from_west_ref[...], 0.0)
    for core in cores:
        planes = core.shape[0] if len(core.shape) == 3 else 1
        for c in range(planes):
            view = core.at[c] if len(core.shape) == 3 else core
            low = pltpu.roll(from_east, (128 - 8 * at) % 128, 1) if at else from_east
            high = pltpu.roll(from_west, (120 - 8 * at) % 128, 1)
            side = jnp.where(lane < 8, low, jnp.where(lane >= 120, high, 0.0))
            side_ref[at] = side
            north_ref[at, :, :COLS] = view[0:8, :]
            north_ref[at, :, COLS:] = side[0:8]
            south_ref[at, :, :COLS] = view[ROWS - 8:ROWS, :]
            south_ref[at, :, COLS:] = side[ROWS - 8:ROWS]
            at += 1


def sweep_kernel(prev_ref, scale_ref, prev_side_ref, prev_south_ref, prev_north_ref,
                 load_ref, load_side_ref, load_south_ref, load_north_ref, mat_ref, msg_ref,
                 out_ref, ret_ref, u_ref, f_ref, inv_ref, x_ref, hl_ref):
    for dst, core, side, south, north in (
        (u_ref, prev_ref, prev_side_ref, prev_south_ref, prev_north_ref),
        (f_ref, load_ref, load_side_ref, load_south_ref, load_north_ref),
    ):
        dst[:, 0:ROWS, 0:COLS] = core[...]
        dst[:, 0:ROWS, COLS:PAD_C] = side[0:12]
        dst[:, ROWS:ROWS + 8, :] = south[0:12]
        dst[:, ROWS + 8:PAD_R, :] = north[0:12]
    inv_ref[0:ROWS, 0:COLS] = scale_ref[...]
    inv_ref[0:ROWS, COLS:PAD_C] = prev_side_ref[12]
    inv_ref[ROWS:ROWS + 8, :] = prev_south_ref[12]
    inv_ref[ROWS + 8:PAD_R, :] = prev_north_ref[12]
    grp, dev = lax.axis_index("grp"), lax.axis_index("dev")
    row, col = iota((PAD_R, PAD_C), 0), iota((PAD_R, PAD_C), 1)
    row_ok = (row < ROWS) | ((row < ROWS + 8) & (grp < lax.axis_size("grp") - 1)) | ((row >= ROWS + 8) & (grp > 0))
    col_ok = (col < COLS) | ((col < COLS + 8) & (dev < lax.axis_size("dev") - 1)) | ((col >= PAD_C - 8) & (dev > 0))
    ok = row_ok & col_ok
    inv_ref[...] = jnp.where(ok, 1.0 / jnp.where(ok, inv_ref[...], 1.0), 0.0)
    for c in range(12):
        u_ref[c] = jnp.where(ok, u_ref[c], 0.0)
    along = ((1, 1), (0, PAD_C - 1), (3, 1), (2, PAD_C - 1))
    across = ((2, 1), (3, 1), (0, PAD_R - 1), (1, PAD_R - 1))

    def sweep(turn, carry):
        for n in range(4):
            for c in range(3):
                at = 3 * n + c
                right = (
                    f_ref[at]
                    + pltpu.roll(u_ref[3 * along[n][0] + c], along[n][1], 1)
                    + pltpu.roll(u_ref[3 * across[n][0] + c], across[n][1], 0)
                )
                top, rest = split(right)
                for b in range(PAD_R // 16):
                    x_ref[b, 16 * at:16 * at + 16] = top[16 * b:16 * b + 16]
                    x_ref[b, 192 + 16 * at:192 + 16 * at + 16] = rest[16 * b:16 * b + 16]
        high = mat_ref[0]
        both = jnp.concatenate([high, high], axis=1)
        for b in range(PAD_R // 16):
            solved = dot(both, x_ref[b]) + dot(mat_ref[1], x_ref[b, 0:192])
            factor = inv_ref[16 * b:16 * b + 16]
            for at in range(12):
                u_ref[at, 16 * b:16 * b + 16] = solved[16 * at:16 * at + 16] * factor
        return carry

    lax.fori_loop(0, SWEEPS, sweep, 0)
    for c in range(12):
        value = u_ref[c, 0:ROWS, 0:COLS]
        out_ref[c] = value
        top, rest = split(value)
        hl_ref[c * ROWS:(c + 1) * ROWS, :COLS] = top
        hl_ref[c * ROWS:(c + 1) * ROWS, COLS:] = rest
    first = iota((8, 128), 1) < 64

    def gather(i, carry):
        markers = []
        for q in range(2):
            even, _ = pair_up(msg_ref[4 * i + 2 * q], msg_ref[4 * i + 2 * q + 1])
            markers.append(even[6:7])
        row, col = element_of(jnp.concatenate(markers, axis=1))
        col_hot = one_hot(iota((COLS, 256), 0) == col)
        row_hot = iota((ROWS, 256), 0) == row
        found = dot(hl_ref[...], jnp.concatenate([col_hot, col_hot], axis=0))
        values = [
            jnp.sum(jnp.where(row_hot, found[c * ROWS:(c + 1) * ROWS], 0.0), axis=0, keepdims=True)
            for c in range(12)
        ]
        for q in range(2):
            lanes = slice(128 * q, 128 * q + 128)
            blank = jnp.zeros((2, 128), F32)
            even = jnp.concatenate([values[c][:, lanes] for c in range(0, 12, 2)] + [blank], axis=0)
            odd = jnp.concatenate([values[c][:, lanes] for c in range(1, 12, 2)] + [blank], axis=0)
            ret_ref[4 * i + 2 * q] = jnp.where(first, even, pltpu.roll(odd, 64, 1))
            ret_ref[4 * i + 2 * q + 1] = jnp.where(first, pltpu.roll(even, 64, 1), odd)
        return carry

    lax.fori_loop(0, OWNERS // 4, gather, 0)


def return_kernel(ret_ref, owner_ref, rank_ref, transfer_ref, out_ref, l_ref):
    for j in range(6):
        top, rest = split(jnp.transpose(ret_ref[:, j, :]))
        l_ref[128 * j:128 * j + 128, :128] = top
        l_ref[128 * j:128 * j + 128, 128:] = rest
    pick = (iota((48, 10), 0) % 16 == iota((48, 10), 1)).astype(F32)
    spread = lax.dot_general(pick, transfer_ref[...], NT, precision=HIGHEST, preferred_element_type=F32)
    spread = exact(spread, (iota((4, 12), 1) // 3 == iota((4, 12), 0)).astype(F32))
    spread = jnp.where(iota((48, 12), 0) // 16 == iota((48, 12), 1) % 3, spread, 0.0)

    def body(i, carry):
        part = pl.ds(pl.multiple_of(i * CHUNK, CHUNK), CHUNK)
        hot = one_hot(iota((OWNERS, CHUNK), 0) == owner_ref[:, part])
        place = iota((CAP, CHUNK), 0).astype(F32) == rank_ref[:, part]
        found = dot(l_ref[...], jnp.concatenate([hot, hot], axis=0))
        node = jnp.concatenate(
            [
                jnp.sum(jnp.where(place, found[c * CAP:(c + 1) * CAP], 0.0), axis=0, keepdims=True)
                for c in range(12)
            ],
            axis=0,
        )
        result = exact(spread, node)
        for c in range(3):
            out_ref[c, :, part] = result[16 * c:16 * c + 10]
        return carry

    lax.fori_loop(0, FACES // CHUNK, body, 0)


def call(kernel, outs, scratch, *args):
    single = not isinstance(outs, (list, tuple))
    shapes = [outs] if single else list(outs)
    result = pl.pallas_call(
        kernel,
        out_shape=shapes,
        in_specs=[pl.BlockSpec(memory_space=pltpu.VMEM)] * len(args),
        out_specs=[pl.BlockSpec(memory_space=pltpu.VMEM)] * len(shapes),
        scratch_shapes=scratch,
        compiler_params=pltpu.CompilerParams(vmem_limit_bytes=48 * 1024 * 1024),
    )(*args)
    return result[0] if single else result


def arr(*shape, dtype=F32):
    return jax.ShapeDtypeStruct(shape, dtype)


def ring(axis, step):
    count = lax.axis_size(axis)
    return [(i, (i + step) % count) for i in range(count)]


def shift_pair(toward_low, toward_high, axis):
    return lax.ppermute(toward_low, axis, ring(axis, -1)), lax.ppermute(toward_high, axis, ring(axis, 1))


def rows_call(count, cores, from_east, from_west):
    def kernel(*refs):
        rows_kernel(len(cores), refs)

    return call(
        kernel, [arr(count, ROWS, 128), arr(count, 8, PAD_C), arr(count, 8, PAD_C)], [], *cores, from_east, from_west
    )


def local(face_owner, face_element, element_state, lift, face_scale, transfer, stiffness_ref, element_scale, displacement_prev):
    owner = face_owner.reshape(1, FACES)
    element = face_element.reshape(1, FACES)
    scale = face_scale.reshape(1, FACES)
    prev = displacement_prev.reshape(12, ROWS, COLS)

    msg, rank = call(
        face_kernel,
        [arr(OWNERS, 8, 128), arr(1, FACES)],
        [pltpu.VMEM((14 * CAP, 2 * CHUNK), BF16), pltpu.VMEM((OWNERS, 14 * CAP), F32)],
        owner, element, element_state, scale, lift, transfer,
    )
    got = lax.all_to_all(msg, ("grp", "dev"), split_axis=0, concat_axis=0)

    west, east, mat = call(
        edge_kernel, [arr(ROWS, 128), arr(ROWS, 128), arr(2, 192, 192, dtype=BF16)], [], prev, element_scale, stiffness_ref
    )
    from_east, from_west = shift_pair(west, east, "dev")
    prev_side, north, south = rows_call(13, [prev, element_scale], from_east, from_west)
    prev_south, prev_north = shift_pair(north, south, "grp")

    load, west, east = call(
        scatter_kernel,
        [arr(12, ROWS, COLS), arr(ROWS, 128), arr(ROWS, 128)],
        [
            pltpu.VMEM((12 * ROWS, 256 * PAIRS), BF16),
            pltpu.VMEM((COLS, 256 * PAIRS), BF16),
            pltpu.VMEM((12 * ROWS, COLS), F32),
        ],
        got,
    )
    from_east, from_west = shift_pair(west, east, "dev")
    load_side, north, south = rows_call(12, [load], from_east, from_west)
    load_south, load_north = shift_pair(north, south, "grp")

    shell, back = call(
        sweep_kernel,
        [arr(12, ROWS, COLS), arr(OWNERS, 8, 128)],
        [
            pltpu.VMEM((12, PAD_R, PAD_C), F32),
            pltpu.VMEM((12, PAD_R, PAD_C), F32),
            pltpu.VMEM((PAD_R, PAD_C), F32),
            pltpu.VMEM((PAD_R // 16, 384, PAD_C), BF16),
            pltpu.VMEM((12 * ROWS, 2 * COLS), BF16),
        ],
        prev, element_scale, prev_side, prev_south, prev_north,
        load, load_side, load_south, load_north, mat, got,
    )
    returned = lax.all_to_all(back, ("grp", "dev"), split_axis=0, concat_axis=0)
    faces = call(
        return_kernel, arr(3, 10, FACES), [pltpu.VMEM((12 * CAP, 256), BF16)], returned, owner, rank, transfer
    )
    return shell.reshape(4, 3, ROWS, COLS), faces


def solution(mesh):
    placed = (
        P(("grp", "dev"), None),
        P(("grp", "dev")),
        P(None, ("grp", "dev")),
        P(),
        P(("grp", "dev")),
        P(),
        P(),
        P("grp", "dev"),
        P(None, None, "grp", "dev"),
    )
    return jax.shard_map(
        local,
        mesh=mesh,
        in_specs=placed,
        out_specs=(P(None, None, "grp", "dev"), P(None, None, ("grp", "dev"))),
        check_vma=False,
    )
```

```python
import functools

import jax
import jax.numpy as jnp
from jax import lax
from jax.experimental import pallas as pl
from jax.experimental.pallas import tpu as pltpu
from jax.sharding import PartitionSpec as P

SWEEPS = 8
WEIGHT = 2.2
HIGHEST = lax.Precision.HIGHEST
F32 = jnp.float32
BF16 = jnp.bfloat16
I32 = jnp.int32

OWNERS = 128
CAP = 64
COLS = 256
ROWS = 64
PAD_R = 80
PAD_C = 384
FACES = 4096
CHUNK = 256
STEP = 1024
HALF = 32
NT = (((1,), (1,)), ((), ()))


def iota(shape, dim):
    return lax.broadcasted_iota(I32, shape, dim)


def dot(a, b):
    return jnp.dot(a, b, preferred_element_type=F32)


def dot_nt(a, b):
    return lax.dot_general(a, b, NT, preferred_element_type=F32)


def exact(a, b):
    return jnp.dot(a, b, precision=HIGHEST, preferred_element_type=F32)


def one_hot(flag):
    return flag.astype(F32).astype(BF16)


def split(x):
    high = x.astype(BF16)
    return high, (x - high.astype(F32)).astype(BF16)


def hot_rows(row, count):
    wide = jnp.broadcast_to(row, (16, row.shape[1]))
    step = iota((16, row.shape[1]), 0).astype(F32)
    return jnp.concatenate([one_hot(step == wide - 16.0 * k) for k in range(count // 16)], axis=0)


def quarters(hot, quarter):
    wide = jnp.broadcast_to(quarter, (16, quarter.shape[1]))
    return [hot * jnp.concatenate([one_hot(wide == q)] * (OWNERS // 16), axis=0) for q in range(4)]


def face_kernel(owner_ref, elem_ref, state_ref, scale_ref, lift_ref, transfer_ref, west_ref, msg_ref, rank_ref,
                x_ref, hot_ref, acc_ref):
    del west_ref
    by_node = exact((iota((12, 4), 0) // 3 == iota((12, 4), 1)).astype(F32), transfer_ref[...])
    spread = exact(by_node, (iota((10, 30), 1) % 10 == iota((10, 30), 0)).astype(F32))
    spread = jnp.where(iota((12, 30), 0) % 3 == iota((12, 30), 1) // 10, spread, 0.0)
    weights = exact(spread, lift_ref[...].astype(F32))
    high, low = split(weights)
    x_ref[...] = jnp.zeros_like(x_ref)
    acc_ref[...] = jnp.zeros_like(acc_ref)
    before = iota((CHUNK, 2 * CHUNK), 0)
    upper = iota((CHUNK, 2 * CHUNK), 1)
    upper = one_hot((before < upper) | (upper >= CHUNK))

    def ranks(i, base):
        part = pl.ds(pl.multiple_of(i * CHUNK, CHUNK), CHUNK)
        hot = (iota((OWNERS, CHUNK), 0) == owner_ref[:, part]).astype(F32)
        counts = dot(hot.astype(BF16), upper)
        rank_ref[:, part] = jnp.sum(hot * (counts[:, :CHUNK] + base), axis=0, keepdims=True)
        return base + counts[:, CHUNK:]

    lax.fori_loop(0, FACES // CHUNK, ranks, jnp.zeros((OWNERS, CHUNK), F32), unroll=4)

    def body(i, carry):
        part = pl.ds(pl.multiple_of(i * STEP, STEP), STEP)
        rank = rank_ref[:, part].astype(I32)
        hot = hot_rows(owner_ref[:, part].astype(F32), OWNERS)
        for q, piece in enumerate(quarters(hot, rank >> 4)):
            hot_ref[q * OWNERS:(q + 1) * OWNERS, :] = piece
        place = hot_rows((rank & 15).astype(F32), 16)
        state = state_ref[:, part]
        load = (dot(high, state) + dot(low, state)) * scale_ref[:, part]
        marker = (elem_ref[:, part] + 1).astype(F32)
        for c in range(13):
            row = load[c:c + 1] if c < 12 else marker
            top, rest = split(jnp.broadcast_to(row, (16, STEP)))
            x_ref[16 * c:16 * c + 16, :STEP] = place * top
            x_ref[16 * c:16 * c + 16, STEP:] = place * rest
        acc_ref[...] += dot_nt(hot_ref[...], x_ref[:, :STEP]) + dot_nt(hot_ref[...], x_ref[:, STEP:])
        return carry

    lax.fori_loop(0, FACES // STEP, body, 0)
    for q in range(4):
        for t in range(2):
            msg_ref[:, 2 * q + t, :] = acc_ref[q * OWNERS:(q + 1) * OWNERS, 128 * t:128 * t + 128]


def places(marker):
    element = marker.astype(I32) - 1
    row, col = element >> 8, (element & 255).astype(F32)
    columns = jnp.concatenate(
        [hot_rows(jnp.where(row < HALF, col, -1.0), COLS), hot_rows(jnp.where(row < HALF, -1.0, col), COLS)], axis=0
    )
    return (row & (HALF - 1)).astype(F32), columns


def edge_sends(comps, west_ref, east_ref):
    lane = iota((ROWS, 128), 1)
    west = jnp.zeros((ROWS, 128), F32)
    east = jnp.zeros((ROWS, 128), F32)
    for i, comp in enumerate(comps):
        here = lane // 8 == i
        low = comp(0)
        high = comp(128)
        west = jnp.where(here, pltpu.roll(low, 8 * i, 1) if i else low, west)
        east = jnp.where(here, pltpu.roll(high, (8 * i + 8) % 128, 1), east)
    west_ref[...] = west
    east_ref[...] = east


def scatter_kernel(msg_ref, load_ref, west_ref, east_ref, mark_ref, a_ref, col_ref, acc_ref, turned_ref):
    acc_ref[...] = jnp.zeros_like(acc_ref)
    for j in range(8):
        turned_ref[j] = jnp.transpose(msg_ref[:, j, :])
    for q in range(4):
        mark_ref[16 * q:16 * q + 16, :] = turned_ref[2 * q + 1, 64:80, :]

    def body(g, carry):
        q, h = g >> 1, pl.multiple_of(8 * (g & 1), 8)
        markers = mark_ref[pl.ds(pl.multiple_of(8 * g, 8), 8), :]
        for k in range(8):
            lanes = slice(128 * k, 128 * k + 128)
            row, columns = places(markers[k:k + 1])
            col_ref[:, lanes] = columns
            row_hot = hot_rows(row, HALF)
            for c in range(12):
                values = turned_ref[2 * q + c // 8, pl.ds(16 * (c % 8) + h, 8), :]
                top, rest = split(jnp.broadcast_to(values[k:k + 1] * (1.0 / WEIGHT), (16, 128)))
                for b in range(HALF // 16):
                    at = c * HALF + 16 * b
                    a_ref[at:at + 16, lanes] = row_hot[16 * b:16 * b + 16] * top
                    a_ref[at:at + 16, 1024 + 128 * k:1024 + 128 * k + 128] = row_hot[16 * b:16 * b + 16] * rest
        acc_ref[...] += dot_nt(a_ref[:, :1024], col_ref[...]) + dot_nt(a_ref[:, 1024:], col_ref[...])
        return carry

    lax.fori_loop(0, 8, body, 0)
    for c in range(12):
        for b in range(2):
            load_ref[c, HALF * b:HALF * (b + 1), :] = acc_ref[c * HALF:(c + 1) * HALF, COLS * b:COLS * (b + 1)]
    edge_sends([(lambda lane, c=c: load_ref[c, :, lane:lane + 128]) for c in range(12)], west_ref, east_ref)


def edge_kernel(prev_ref, scale_ref, west_ref, east_ref):
    comps = [(lambda lane, c=c: prev_ref[c, :, lane:lane + 128]) for c in range(12)]
    comps.append(lambda lane: scale_ref[:, lane:lane + 128])
    edge_sends(comps, west_ref, east_ref)


def matrix_kernel(stiff_ref, mat_ref):
    eye = (iota((12, 12), 0) == iota((12, 12), 1)).astype(F32)
    approx = eye / 5.0
    rest = eye - exact(stiff_ref[...], approx)
    for turn in range(8):
        approx = approx + exact(approx, rest)
        if turn < 7:
            rest = exact(rest, rest)
    tall = (iota((192, 12), 0) // 16 == iota((192, 12), 1)).astype(F32)
    wide = (iota((12, 192), 1) // 16 == iota((12, 192), 0)).astype(F32)
    big = exact(exact(tall, approx * WEIGHT), wide)
    big = jnp.where(iota((192, 192), 0) % 16 == iota((192, 192), 1) % 16, big, 0.0)
    high, low = split(big)
    mat_ref[0] = high
    mat_ref[1] = low


def rows_kernel(count, refs):
    cores, (from_east_ref, from_west_ref, side_ref, north_ref, south_ref) = refs[:count], refs[count:]
    at = 0
    lane = iota((ROWS, 128), 1)
    dev = lax.axis_index("dev")
    from_east = jnp.where(dev < lax.axis_size("dev") - 1, from_east_ref[...], 0.0)
    from_west = jnp.where(dev > 0, from_west_ref[...], 0.0)
    for core in cores:
        planes = core.shape[0] if len(core.shape) == 3 else 1
        for c in range(planes):
            view = core.at[c] if len(core.shape) == 3 else core
            low = pltpu.roll(from_east, (128 - 8 * at) % 128, 1) if at else from_east
            high = pltpu.roll(from_west, (120 - 8 * at) % 128, 1)
            side = jnp.where(lane < 8, low, jnp.where(lane >= 120, high, 0.0))
            side_ref[at] = side
            north_ref[at, :, :COLS] = view[0:8, :]
            north_ref[at, :, COLS:] = side[0:8]
            south_ref[at, :, :COLS] = view[ROWS - 8:ROWS, :]
            south_ref[at, :, COLS:] = side[ROWS - 8:ROWS]
            at += 1


def sweep_kernel(prev_ref, scale_ref, prev_side_ref, prev_south_ref, prev_north_ref,
                 load_ref, load_side_ref, load_south_ref, load_north_ref, mat_ref, mark_ref,
                 out_ref, ret_ref, u_ref, f_ref, inv_ref, x_ref, hl_ref, turned_ref):
    for dst, core, side, south, north in (
        (u_ref, prev_ref, prev_side_ref, prev_south_ref, prev_north_ref),
        (f_ref, load_ref, load_side_ref, load_south_ref, load_north_ref),
    ):
        dst[:, 0:ROWS, 0:COLS] = core[...]
        dst[:, 0:ROWS, COLS:PAD_C] = side[0:12]
        dst[:, ROWS:ROWS + 8, :] = south[0:12]
        dst[:, ROWS + 8:PAD_R, :] = north[0:12]
    inv_ref[0:ROWS, 0:COLS] = scale_ref[...]
    inv_ref[0:ROWS, COLS:PAD_C] = prev_side_ref[12]
    inv_ref[ROWS:ROWS + 8, :] = prev_south_ref[12]
    inv_ref[ROWS + 8:PAD_R, :] = prev_north_ref[12]
    grp, dev = lax.axis_index("grp"), lax.axis_index("dev")
    row, col = iota((PAD_R, PAD_C), 0), iota((PAD_R, PAD_C), 1)
    row_ok = (row < ROWS) | ((row < ROWS + 8) & (grp < lax.axis_size("grp") - 1)) | ((row >= ROWS + 8) & (grp > 0))
    col_ok = (col < COLS) | ((col < COLS + 8) & (dev < lax.axis_size("dev") - 1)) | ((col >= PAD_C - 8) & (dev > 0))
    ok = row_ok & col_ok
    inv_ref[...] = jnp.where(ok, 1.0 / jnp.where(ok, inv_ref[...], 1.0), 0.0)
    for c in range(12):
        u_ref[c] = jnp.where(ok, u_ref[c], 0.0)
    along = ((1, 1), (0, PAD_C - 1), (3, 1), (2, PAD_C - 1))
    across = ((2, 1), (3, 1), (0, PAD_R - 1), (1, PAD_R - 1))

    def sweep(turn, carry):
        for n in range(4):
            for c in range(3):
                at = 3 * n + c
                right = (
                    f_ref[at]
                    + pltpu.roll(u_ref[3 * along[n][0] + c], along[n][1], 1)
                    + pltpu.roll(u_ref[3 * across[n][0] + c], across[n][1], 0)
                )
                top, rest = split(right)
                for b in range(PAD_R // 16):
                    x_ref[b, 16 * at:16 * at + 16] = top[16 * b:16 * b + 16]
                    x_ref[b, 192 + 16 * at:192 + 16 * at + 16] = rest[16 * b:16 * b + 16]
        high = mat_ref[0]
        both = jnp.concatenate([high, high], axis=1)
        for b in range(PAD_R // 16):
            solved = dot(both, x_ref[b]) + dot(mat_ref[1], x_ref[b, 0:192])
            factor = inv_ref[16 * b:16 * b + 16]
            for at in range(12):
                u_ref[at, 16 * b:16 * b + 16] = solved[16 * at:16 * at + 16] * factor
        return carry

    lax.fori_loop(0, SWEEPS, sweep, 0)
    for c in range(12):
        value = u_ref[c, 0:ROWS, 0:COLS]
        out_ref[c] = value
        top, rest = split(value)
        for b in range(2):
            part = slice(HALF * b, HALF * (b + 1))
            hl_ref[c * HALF:(c + 1) * HALF, COLS * b:COLS * (b + 1)] = top[part]
            hl_ref[c * HALF:(c + 1) * HALF, 512 + COLS * b:512 + COLS * (b + 1)] = rest[part]

    def gather(g, carry):
        q, h = g >> 1, pl.multiple_of(8 * (g & 1), 8)
        markers = mark_ref[pl.ds(pl.multiple_of(8 * g, 8), 8), :]
        for s in range(2):
            row, columns = places(jnp.concatenate([markers[4 * s + k:4 * s + k + 1] for k in range(4)], axis=1))
            found = dot(hl_ref[:, :512], columns) + dot(hl_ref[:, 512:], columns)
            here = iota((HALF, 512), 0).astype(F32) == row
            for c in range(12):
                value = jnp.sum(jnp.where(here, found[c * HALF:(c + 1) * HALF], 0.0), axis=0, keepdims=True)
                value = jnp.concatenate([value[:, 128 * k:128 * k + 128] for k in range(4)], axis=0)
                turned_ref[2 * q + c // 8, pl.ds(16 * (c % 8) + h + 4 * s, 4), :] = value
        return carry

    lax.fori_loop(0, 8, gather, 0)
    for j in range(8):
        ret_ref[:, j, :] = jnp.transpose(turned_ref[j])


def return_kernel(ret_ref, owner_ref, rank_ref, transfer_ref, out_ref, l_ref, hot_ref, faces_ref, sems):
    for q in range(4):
        for t in range(2):
            count = 128 if t == 0 else 64
            top, rest = split(jnp.transpose(ret_ref[:, 2 * q + t, :])[:count])
            l_ref[128 * t:128 * t + count, 128 * q:128 * q + 128] = top
            l_ref[128 * t:128 * t + count, 512 + 128 * q:512 + 128 * q + 128] = rest
    pick = (iota((48, 10), 0) % 16 == iota((48, 10), 1)).astype(F32)
    spread = lax.dot_general(pick, transfer_ref[...], NT, precision=HIGHEST, preferred_element_type=F32)
    spread = exact(spread, (iota((4, 16), 1) // 3 == iota((4, 16), 0)).astype(F32))
    spread = jnp.where(iota((48, 16), 0) // 16 == iota((48, 16), 1) % 3, spread, 0.0)
    high, low = split(spread)
    copies = []
    for i in range(FACES // STEP):
        part = slice(i * STEP, (i + 1) * STEP)
        rank = rank_ref[:, part].astype(I32)
        hot = hot_rows(owner_ref[:, part].astype(F32), OWNERS)
        for q, piece in enumerate(quarters(hot, rank >> 4)):
            hot_ref[q * OWNERS:(q + 1) * OWNERS, :] = piece
        found = dot(l_ref[:, :512], hot_ref[...]) + dot(l_ref[:, 512:], hot_ref[...])
        here = iota((16, STEP), 0) == (rank & 15)
        node = jnp.concatenate(
            [jnp.sum(jnp.where(here, found[16 * c:16 * c + 16], 0.0), axis=0, keepdims=True) for c in range(12)]
            + [jnp.zeros((4, STEP), F32)],
            axis=0,
        )
        top, rest = split(node)
        result = dot(high, top) + (dot(high, rest) + dot(low, top))
        for c in range(3):
            faces_ref[c, :, part] = result[16 * c:16 * c + 10]
        copy = pltpu.make_async_copy(faces_ref.at[:, :, part], out_ref.at[:, :, part], sems.at[i])
        copy.start()
        copies.append(copy)
    for copy in copies:
        copy.wait()


VMEM = pl.BlockSpec(memory_space=pltpu.VMEM)
HBM = pl.BlockSpec(memory_space=pl.ANY)
AUTO = pl.BlockSpec()


def call(kernel, outs, scratch, *args, auto=(), out_specs=None):
    single = not isinstance(outs, (list, tuple))
    shapes = [outs] if single else list(outs)
    result = pl.pallas_call(
        kernel,
        out_shape=shapes,
        in_specs=[AUTO if i in auto else VMEM for i in range(len(args))],
        out_specs=out_specs or [VMEM] * len(shapes),
        scratch_shapes=scratch,
        compiler_params=pltpu.CompilerParams(vmem_limit_bytes=48 * 1024 * 1024),
    )(*args)
    return result[0] if single else result


def arr(*shape, dtype=F32):
    return jax.ShapeDtypeStruct(shape, dtype)


def ring(axis, step):
    count = lax.axis_size(axis)
    return [(i, (i + step) % count) for i in range(count)]


def shift_pair(toward_low, toward_high, axis):
    return lax.ppermute(toward_low, axis, ring(axis, -1)), lax.ppermute(toward_high, axis, ring(axis, 1))


def rows_call(count, cores, from_east, from_west):
    def kernel(*refs):
        rows_kernel(len(cores), refs)

    return call(
        kernel, [arr(count, ROWS, 128), arr(count, 8, PAD_C), arr(count, 8, PAD_C)], [], *cores, from_east, from_west
    )


def local(face_owner, face_element, element_state, lift, face_scale, transfer, stiffness_ref, element_scale, displacement_prev):
    owner = face_owner.reshape(1, FACES)
    element = face_element.reshape(1, FACES)
    scale = face_scale.reshape(1, FACES)
    prev = displacement_prev.reshape(12, ROWS, COLS)

    west, east = call(edge_kernel, [arr(ROWS, 128), arr(ROWS, 128)], [], prev, element_scale, auto=(0, 1))
    from_east, from_west = shift_pair(west, east, "dev")
    msg, rank = call(
        face_kernel,
        [arr(OWNERS, 8, 128), arr(1, FACES)],
        [pltpu.VMEM((256, 2 * STEP), BF16), pltpu.VMEM((4 * OWNERS, STEP), BF16), pltpu.VMEM((4 * OWNERS, 256), F32)],
        owner, element, element_state, scale, lift, transfer, west,
        auto=(0, 1, 2, 3, 4, 5),
    )
    prev_side, north, south = rows_call(13, [prev, element_scale], from_east, from_west)
    msg, north, south = lax.optimization_barrier((msg, north, south))
    prev_south, prev_north = shift_pair(north, south, "grp")
    got = lax.all_to_all(msg, ("grp", "dev"), split_axis=0, concat_axis=0)
    mat = call(matrix_kernel, arr(2, 192, 192, dtype=BF16), [], stiffness_ref)

    load, west, east, mark = call(
        scatter_kernel,
        [arr(12, ROWS, COLS), arr(ROWS, 128), arr(ROWS, 128), arr(64, 128)],
        [
            pltpu.VMEM((12 * HALF, 2048), BF16),
            pltpu.VMEM((2 * COLS, 1024), BF16),
            pltpu.VMEM((12 * HALF, 2 * COLS), F32),
            pltpu.VMEM((8, 128, 128), F32),
        ],
        got,
    )
    from_east, from_west = shift_pair(west, east, "dev")
    load_side, north, south = rows_call(12, [load], from_east, from_west)
    load_south, load_north = shift_pair(north, south, "grp")

    shell, back = call(
        sweep_kernel,
        [arr(12, ROWS, COLS), arr(OWNERS, 8, 128)],
        [
            pltpu.VMEM((12, PAD_R, PAD_C), F32),
            pltpu.VMEM((12, PAD_R, PAD_C), F32),
            pltpu.VMEM((PAD_R, PAD_C), F32),
            pltpu.VMEM((PAD_R // 16, 384, PAD_C), BF16),
            pltpu.VMEM((12 * HALF, 1024), BF16),
            pltpu.VMEM((8, 128, 128), F32),
        ],
        prev, element_scale, prev_side, prev_south, prev_north,
        load, load_side, load_south, load_north, mat, mark,
    )
    returned = lax.all_to_all(back, ("grp", "dev"), split_axis=0, concat_axis=0)
    faces = call(
        return_kernel,
        arr(3, 10, FACES),
        [
            pltpu.VMEM((192, 1024), BF16),
            pltpu.VMEM((4 * OWNERS, STEP), BF16),
            pltpu.VMEM((3, 10, FACES), F32),
            pltpu.SemaphoreType.DMA((FACES // STEP,)),
        ],
        returned, owner, rank, transfer,
        out_specs=[HBM],
    )
    return shell.reshape(4, 3, ROWS, COLS), faces


def solution(mesh):
    placed = (
        P(("grp", "dev"), None),
        P(("grp", "dev")),
        P(None, ("grp", "dev")),
        P(),
        P(("grp", "dev")),
        P(),
        P(),
        P("grp", "dev"),
        P(None, None, "grp", "dev"),
    )
    return jax.shard_map(
        local,
        mesh=mesh,
        in_specs=placed,
        out_specs=(P(None, None, "grp", "dev"), P(None, None, ("grp", "dev"))),
        check_vma=False,
    )
```

```python
import functools

import jax
import jax.numpy as jnp
from jax import lax
from jax.experimental import pallas as pl
from jax.experimental.pallas import tpu as pltpu
from jax.sharding import PartitionSpec as P

SWEEPS = 8
WEIGHT = 2.2
HIGHEST = lax.Precision.HIGHEST
F32 = jnp.float32
BF16 = jnp.bfloat16
I32 = jnp.int32

OWNERS = 128
CAP = 64
COLS = 256
ROWS = 64
PAD_R = 80
PAD_C = 384
FACES = 4096
CHUNK = 256
STEP = 1024
HALF = 32
PLANES = 25
LIMIT = 60
NT = (((1,), (1,)), ((), ()))


def iota(shape, dim):
    return lax.broadcasted_iota(I32, shape, dim)


def dot(a, b):
    return jnp.dot(a, b, preferred_element_type=F32)


def dot_nt(a, b):
    return lax.dot_general(a, b, NT, preferred_element_type=F32)


def exact(a, b):
    return jnp.dot(a, b, precision=HIGHEST, preferred_element_type=F32)


def one_hot(flag):
    return flag.astype(F32).astype(BF16)


def split(x):
    high = x.astype(BF16)
    return high, (x - high.astype(F32)).astype(BF16)


def hot_rows(row, count):
    wide = jnp.broadcast_to(row, (16, row.shape[1]))
    step = iota((16, row.shape[1]), 0).astype(F32)
    return jnp.concatenate([one_hot(step == wide - 16.0 * k) for k in range(count // 16)], axis=0)


def quarters(hot, quarter):
    wide = jnp.broadcast_to(quarter, (16, quarter.shape[1]))
    return [hot * jnp.concatenate([one_hot(wide == q)] * (OWNERS // 16), axis=0) for q in range(4)]


def face_kernel(owner_hbm, elem_hbm, state_hbm, scale_hbm, lift_hbm, transfer_hbm, msg_ref, rank_ref,
                owner_ref, elem_ref, state_ref, scale_ref, lift_ref, transfer_ref, x_ref, hot_ref, acc_ref, sems):
    copies = [
        pltpu.make_async_copy(src, dst, sems.at[i])
        for i, (src, dst) in enumerate((
            (owner_hbm, owner_ref), (transfer_hbm, transfer_ref), (lift_hbm, lift_ref),
            (elem_hbm, elem_ref), (scale_hbm, scale_ref), (state_hbm, state_ref),
        ))
    ]
    for copy in copies:
        copy.start()
    x_ref[...] = jnp.zeros_like(x_ref)
    acc_ref[...] = jnp.zeros_like(acc_ref)
    before = iota((CHUNK, 2 * CHUNK), 0)
    upper = iota((CHUNK, 2 * CHUNK), 1)
    upper = one_hot((before < upper) | (upper >= CHUNK))
    copies[0].wait()

    def ranks(i, base):
        part = pl.ds(pl.multiple_of(i * CHUNK, CHUNK), CHUNK)
        hot = (iota((OWNERS, CHUNK), 0) == owner_ref[:, part]).astype(F32)
        counts = dot(hot.astype(BF16), upper)
        rank_ref[:, part] = jnp.sum(hot * (counts[:, :CHUNK] + base), axis=0, keepdims=True)
        return base + counts[:, CHUNK:]

    lax.fori_loop(0, FACES // CHUNK, ranks, jnp.zeros((OWNERS, CHUNK), F32), unroll=4)
    for copy in copies[1:]:
        copy.wait()
    by_node = exact((iota((12, 4), 0) // 3 == iota((12, 4), 1)).astype(F32), transfer_ref[...])
    spread = exact(by_node, (iota((10, 30), 1) % 10 == iota((10, 30), 0)).astype(F32))
    spread = jnp.where(iota((12, 30), 0) % 3 == iota((12, 30), 1) // 10, spread, 0.0)
    weights = exact(spread, lift_ref[...].astype(F32))
    high, low = split(weights)

    def body(i, carry):
        part = pl.ds(pl.multiple_of(i * STEP, STEP), STEP)
        rank = rank_ref[:, part].astype(I32)
        hot = hot_rows(owner_ref[:, part].astype(F32), OWNERS)
        for q, piece in enumerate(quarters(hot, rank >> 4)):
            hot_ref[q * OWNERS:(q + 1) * OWNERS, :] = piece
        place = hot_rows((rank & 15).astype(F32), 16)
        state = state_ref[:, part]
        load = (dot(high, state) + dot(low, state)) * scale_ref[:, part]
        marker = (elem_ref[:, part] + 1).astype(F32)
        for c in range(13):
            row = load[c:c + 1] if c < 12 else marker
            top, rest = split(jnp.broadcast_to(row, (16, STEP)))
            x_ref[16 * c:16 * c + 16, :STEP] = place * top
            x_ref[16 * c:16 * c + 16, STEP:] = place * rest
        acc_ref[...] += dot_nt(hot_ref[...], x_ref[:, :STEP]) + dot_nt(hot_ref[...], x_ref[:, STEP:])
        return carry

    lax.fori_loop(0, FACES // STEP, body, 0)
    for q in range(4):
        for t in range(2):
            msg_ref[:, 2 * q + t, :] = acc_ref[q * OWNERS:(q + 1) * OWNERS, 128 * t:128 * t + 128]


def places(marker):
    element = marker.astype(I32) - 1
    row, col = element >> 8, (element & 255).astype(F32)
    columns = jnp.concatenate(
        [hot_rows(jnp.where(row < HALF, col, -1.0), COLS), hot_rows(jnp.where(row < HALF, -1.0, col), COLS)], axis=0
    )
    return (row & (HALF - 1)).astype(F32), columns


def edge_sends(comps, west_ref, east_ref):
    lane = iota((ROWS, 128), 1)
    for tile in range(2):
        west = jnp.zeros((ROWS, 128), F32)
        east = jnp.zeros((ROWS, 128), F32)
        for i, comp in enumerate(comps[16 * tile:16 * tile + 16]):
            here = lane // 8 == i
            low = comp(0)
            high = comp(128)
            west = jnp.where(here, pltpu.roll(low, 8 * i, 1) if i else low, west)
            east = jnp.where(here, pltpu.roll(high, (8 * i + 8) % 128, 1), east)
        west_ref[:, 128 * tile:128 * tile + 128] = west
        east_ref[:, 128 * tile:128 * tile + 128] = east


def scatter_kernel(msg_ref, prev_ref, scale_ref, load_ref, west_ref, east_ref, mark_ref, a_ref, col_ref, acc_ref, turned_ref):
    acc_ref[...] = jnp.zeros_like(acc_ref)
    for j in range(8):
        turned_ref[j] = jnp.transpose(msg_ref[:, j, :])
    for q in range(4):
        mark_ref[16 * q:16 * q + 16, :] = turned_ref[2 * q + 1, 64:80, :]

    def body(g, carry):
        q, h = g >> 1, pl.multiple_of(8 * (g & 1), 8)
        markers = mark_ref[pl.ds(pl.multiple_of(8 * g, 8), 8), :]
        for k in range(8):
            lanes = slice(128 * k, 128 * k + 128)
            row, columns = places(markers[k:k + 1])
            col_ref[:, lanes] = columns
            row_hot = hot_rows(row, HALF)
            for c in range(12):
                values = turned_ref[2 * q + c // 8, pl.ds(16 * (c % 8) + h, 8), :]
                top, rest = split(jnp.broadcast_to(values[k:k + 1] * (1.0 / WEIGHT), (16, 128)))
                for b in range(HALF // 16):
                    at = c * HALF + 16 * b
                    a_ref[at:at + 16, lanes] = row_hot[16 * b:16 * b + 16] * top
                    a_ref[at:at + 16, 1024 + 128 * k:1024 + 128 * k + 128] = row_hot[16 * b:16 * b + 16] * rest
        acc_ref[...] += dot_nt(a_ref[:, :1024], col_ref[...]) + dot_nt(a_ref[:, 1024:], col_ref[...])
        return carry

    lax.fori_loop(0, 8, body, 0)
    for c in range(12):
        for b in range(2):
            load_ref[c, HALF * b:HALF * (b + 1), :] = acc_ref[c * HALF:(c + 1) * HALF, COLS * b:COLS * (b + 1)]
    edge_sends(
        [(lambda lane, c=c: load_ref[c, :, lane:lane + 128]) for c in range(12)]
        + [(lambda lane, c=c: prev_ref[c, :, lane:lane + 128]) for c in range(12)]
        + [lambda lane: scale_ref[:, lane:lane + 128]],
        west_ref, east_ref,
    )


def matrix_kernel(stiff_ref, mat_ref):
    eye = (iota((12, 12), 0) == iota((12, 12), 1)).astype(F32)
    approx = eye / 5.0
    rest = eye - exact(stiff_ref[...], approx)
    for turn in range(8):
        approx = approx + exact(approx, rest)
        if turn < 7:
            rest = exact(rest, rest)
    tall = (iota((96, 12), 0) // 8 == iota((96, 12), 1)).astype(F32)
    wide = (iota((12, 96), 1) // 8 == iota((12, 96), 0)).astype(F32)
    big = exact(exact(tall, approx * WEIGHT), wide)
    big = jnp.where(iota((96, 96), 0) % 8 == iota((96, 96), 1) % 8, big, 0.0)
    high, low = split(big)
    mat_ref[0:96, :] = jnp.concatenate([high, high], axis=1)
    mat_ref[96:192, :] = jnp.concatenate([low, jnp.zeros_like(low)], axis=1)


def rows_kernel(load_ref, prev_ref, scale_ref, from_east_ref, from_west_ref, side_ref, north_ref, south_ref):
    lane = iota((ROWS, 128), 1)
    group = iota((8, 128), 1) // 16
    packed = [[jnp.zeros((8, 128), F32) for _ in range(4)] for _ in range(2)]
    for p in range(PLANES):
        tile = slice(128 * (p // 16), 128 * (p // 16) + 128)
        low = pltpu.roll(from_east_ref[:, tile], (128 - 8 * (p % 16)) % 128, 1)
        high = pltpu.roll(from_west_ref[:, tile], (248 - 8 * (p % 16)) % 128, 1)
        side = jnp.where(lane < 8, low, jnp.where(lane >= 120, high, 0.0))
        side_ref[p] = side
        core = load_ref.at[p] if p < 12 else prev_ref.at[p - 12] if p < 24 else scale_ref
        for way, (ref, at) in enumerate(((north_ref, 0), (south_ref, ROWS - 8))):
            ref[p] = core[at:at + 8, :]
            turned = pltpu.roll(side[at:at + 8], (8 + 16 * (p % 8)) % 128, 1)
            packed[way][p // 8] = jnp.where(group == p % 8, turned, packed[way][p // 8])
    for way, ref in enumerate((north_ref, south_ref)):
        for t in range(4):
            ref[PLANES + t // 2, :, 128 * (t % 2):128 * (t % 2) + 128] = packed[way][t]


def side_of(rows_ref, p):
    t = p // 8
    tile = rows_ref[PLANES + t // 2, :, 128 * (t % 2):128 * (t % 2) + 128]
    return pltpu.roll(tile, (248 - 16 * (p % 8)) % 128, 1)


def sweep_kernel(load_ref, prev_ref, scale_ref, side_ref, south_ref, north_ref, mat_ref, mark_ref,
                 out_ref, ret_ref, u_ref, f_ref, inv_ref, x_ref, hl_ref, turned_ref):
    for p in range(PLANES):
        dst = f_ref.at[p] if p < 12 else u_ref.at[p - 12] if p < 24 else inv_ref
        dst[0:ROWS, 0:COLS] = scale_ref[...] if p == 24 else load_ref[p] if p < 12 else prev_ref[p - 12]
        dst[0:ROWS, COLS:PAD_C] = side_ref[p]
        for at, rows in ((ROWS, south_ref), (ROWS + 8, north_ref)):
            dst[at:at + 8, 0:COLS] = rows[p]
            dst[at:at + 8, COLS:PAD_C] = side_of(rows, p)
    grp, dev = lax.axis_index("grp"), lax.axis_index("dev")
    row, col = iota((PAD_R, PAD_C), 0), iota((PAD_R, PAD_C), 1)
    row_ok = (row < ROWS) | ((row < ROWS + 8) & (grp < lax.axis_size("grp") - 1)) | ((row >= ROWS + 8) & (grp > 0))
    col_ok = (col < COLS) | ((col < COLS + 8) & (dev < lax.axis_size("dev") - 1)) | ((col >= PAD_C - 8) & (dev > 0))
    ok = row_ok & col_ok
    inv_ref[...] = jnp.where(ok, 1.0 / jnp.where(ok, inv_ref[...], 1.0), 0.0)
    for c in range(12):
        u_ref[c] = jnp.where(ok, u_ref[c], 0.0)
    along = ((1, 1), (0, PAD_C - 1), (3, 1), (2, PAD_C - 1))
    across = ((2, 1), (3, 1), (0, PAD_R - 1), (1, PAD_R - 1))

    def right_side(at):
        n, c = divmod(at, 3)
        return (
            f_ref[at]
            + pltpu.roll(u_ref[3 * along[n][0] + c], along[n][1], 1)
            + pltpu.roll(u_ref[3 * across[n][0] + c], across[n][1], 0)
        )

    def sweep(turn, carry):
        for at in range(0, 12, 2):
            first, second = right_side(at), right_side(at + 1)
            for b in range(PAD_R // 8):
                rows = slice(8 * b, 8 * b + 8)
                top, rest = split(jnp.concatenate([first[rows], second[rows]], axis=0))
                lanes = slice(PAD_C * (b % 2), PAD_C * (b % 2) + PAD_C)
                x_ref[b // 2, 8 * at:8 * at + 16, lanes] = top
                x_ref[b // 2, 96 + 8 * at:96 + 8 * at + 16, lanes] = rest
        for b in range(PAD_R // 16):
            solved = dot(mat_ref[...], x_ref[b])
            for h in range(2):
                rows = slice(16 * b + 8 * h, 16 * b + 8 * h + 8)
                lanes = slice(PAD_C * h, PAD_C * h + PAD_C)
                factor = inv_ref[rows]
                for at in range(12):
                    u_ref[at, rows] = (
                        solved[8 * at:8 * at + 8, lanes] + solved[96 + 8 * at:96 + 8 * at + 8, lanes]
                    ) * factor
        return carry

    lax.fori_loop(0, SWEEPS, sweep, 0, unroll=2)
    for c in range(12):
        value = u_ref[c, 0:ROWS, 0:COLS]
        out_ref[c] = value
        top, rest = split(value)
        for b in range(2):
            part = slice(HALF * b, HALF * (b + 1))
            hl_ref[c * HALF:(c + 1) * HALF, COLS * b:COLS * (b + 1)] = top[part]
            hl_ref[c * HALF:(c + 1) * HALF, 512 + COLS * b:512 + COLS * (b + 1)] = rest[part]

    def gather(g, carry):
        q, h = g >> 1, pl.multiple_of(8 * (g & 1), 8)
        markers = mark_ref[pl.ds(pl.multiple_of(8 * g, 8), 8), :]
        for s in range(2):
            row, columns = places(jnp.concatenate([markers[4 * s + k:4 * s + k + 1] for k in range(4)], axis=1))
            found = dot(hl_ref[:, :512], columns) + dot(hl_ref[:, 512:], columns)
            here = iota((HALF, 512), 0).astype(F32) == row
            for c in range(12):
                value = jnp.sum(jnp.where(here, found[c * HALF:(c + 1) * HALF], 0.0), axis=0, keepdims=True)
                value = jnp.concatenate([value[:, 128 * k:128 * k + 128] for k in range(4)], axis=0)
                turned_ref[2 * q + c // 8, pl.ds(16 * (c % 8) + h + 4 * s, 4), :] = value
        return carry

    lax.fori_loop(0, 8, gather, 0)
    for j in range(8):
        ret_ref[:, j, :] = jnp.transpose(turned_ref[j])


def return_kernel(ret_ref, owner_ref, rank_ref, transfer_ref, out_ref, l_ref, hot_ref, faces_ref, sems):
    for q in range(4):
        for t in range(2):
            count = 128 if t == 0 else 64
            top, rest = split(jnp.transpose(ret_ref[:, 2 * q + t, :])[:count])
            l_ref[128 * t:128 * t + count, 128 * q:128 * q + 128] = top
            l_ref[128 * t:128 * t + count, 512 + 128 * q:512 + 128 * q + 128] = rest
    pick = (iota((80, 10), 0) // 8 == iota((80, 10), 1)).astype(F32)
    spread = lax.dot_general(pick, transfer_ref[...], NT, precision=HIGHEST, preferred_element_type=F32)
    spread = exact(spread, (iota((4, 16), 1) // 3 == iota((4, 16), 0)).astype(F32))
    spread = jnp.where(iota((80, 16), 0) % 8 == iota((80, 16), 1) % 3, spread, 0.0)
    high, low = split(spread)
    copies = []
    for i in range(FACES // STEP):
        part = slice(i * STEP, (i + 1) * STEP)
        rank = rank_ref[:, part].astype(I32)
        hot = hot_rows(owner_ref[:, part].astype(F32), OWNERS)
        for q, piece in enumerate(quarters(hot, rank >> 4)):
            hot_ref[q * OWNERS:(q + 1) * OWNERS, :] = piece
        found = dot(l_ref[:, :512], hot_ref[...]) + dot(l_ref[:, 512:], hot_ref[...])
        here = iota((16, STEP), 0) == (rank & 15)
        node = jnp.concatenate(
            [jnp.sum(jnp.where(here, found[16 * c:16 * c + 16], 0.0), axis=0, keepdims=True) for c in range(12)]
            + [jnp.zeros((4, STEP), F32)],
            axis=0,
        )
        top, rest = split(node)
        result = dot(high, top) + (dot(high, rest) + dot(low, top))
        for k in range(10):
            faces_ref[k, :, part] = result[8 * k:8 * k + 3]
        copy = pltpu.make_async_copy(faces_ref.at[:, :, part], out_ref.at[:, :, part], sems.at[i])
        copy.start()
        copies.append(copy)
    for copy in copies:
        copy.wait()


VMEM = pl.BlockSpec(memory_space=pltpu.VMEM)
HBM = pl.BlockSpec(memory_space=pl.ANY)


def call(kernel, outs, scratch, *args, hbm=(), out_specs=None, limit=48):
    single = not isinstance(outs, (list, tuple))
    shapes = [outs] if single else list(outs)
    result = pl.pallas_call(
        kernel,
        out_shape=shapes,
        in_specs=[HBM if i in hbm else VMEM for i in range(len(args))],
        out_specs=out_specs or [VMEM] * len(shapes),
        scratch_shapes=scratch,
        compiler_params=pltpu.CompilerParams(vmem_limit_bytes=limit * 1024 * 1024),
    )(*args)
    return result[0] if single else result


def arr(*shape, dtype=F32):
    return jax.ShapeDtypeStruct(shape, dtype)


def ring(axis, step):
    count = lax.axis_size(axis)
    return [(i, (i + step) % count) for i in range(count)]


def shift_pair(toward_low, toward_high, axis):
    return lax.ppermute(toward_low, axis, ring(axis, -1)), lax.ppermute(toward_high, axis, ring(axis, 1))


def local(face_owner, face_element, element_state, lift, face_scale, transfer, stiffness_ref, element_scale, displacement_prev):
    owner = face_owner.reshape(1, FACES)
    element = face_element.reshape(1, FACES)
    scale = face_scale.reshape(1, FACES)
    prev = displacement_prev.reshape(12, ROWS, COLS)

    msg, rank = call(
        face_kernel,
        [arr(OWNERS, 8, 128), arr(1, FACES)],
        [
            pltpu.VMEM((1, FACES), I32), pltpu.VMEM((1, FACES), I32), pltpu.VMEM((110, FACES), BF16),
            pltpu.VMEM((1, FACES), F32), pltpu.VMEM((30, 110), BF16), pltpu.VMEM((4, 10), F32),
            pltpu.VMEM((256, 2 * STEP), BF16), pltpu.VMEM((4 * OWNERS, STEP), BF16), pltpu.VMEM((4 * OWNERS, 256), F32),
            pltpu.SemaphoreType.DMA((6,)),
        ],
        owner, element, element_state, scale, lift, transfer,
        hbm=(0, 1, 2, 3, 4, 5), limit=LIMIT,
    )
    got = lax.all_to_all(msg, ("grp", "dev"), split_axis=0, concat_axis=0)
    mat = call(matrix_kernel, arr(192, 192, dtype=BF16), [], stiffness_ref)

    load, west, east, mark = call(
        scatter_kernel,
        [arr(12, ROWS, COLS), arr(ROWS, 256), arr(ROWS, 256), arr(64, 128)],
        [
            pltpu.VMEM((12 * HALF, 2048), BF16),
            pltpu.VMEM((2 * COLS, 1024), BF16),
            pltpu.VMEM((12 * HALF, 2 * COLS), F32),
            pltpu.VMEM((8, 128, 128), F32),
        ],
        got, prev, element_scale,
    )
    from_east, from_west = shift_pair(west, east, "dev")
    side, north, south = call(
        rows_kernel,
        [arr(PLANES, ROWS, 128), arr(PLANES + 2, 8, COLS), arr(PLANES + 2, 8, COLS)],
        [],
        load, prev, element_scale, from_east, from_west,
    )
    south, north = shift_pair(north, south, "grp")

    shell, back = call(
        sweep_kernel,
        [arr(12, ROWS, COLS), arr(OWNERS, 8, 128)],
        [
            pltpu.VMEM((12, PAD_R, PAD_C), F32),
            pltpu.VMEM((12, PAD_R, PAD_C), F32),
            pltpu.VMEM((PAD_R, PAD_C), F32),
            pltpu.VMEM((PAD_R // 16, 192, 2 * PAD_C), BF16),
            pltpu.VMEM((12 * HALF, 1024), BF16),
            pltpu.VMEM((8, 128, 128), F32),
        ],
        load, prev, element_scale, side, south, north, mat, mark,
    )
    returned = lax.all_to_all(back, ("grp", "dev"), split_axis=0, concat_axis=0)
    faces = call(
        return_kernel,
        arr(10, 3, FACES),
        [
            pltpu.VMEM((192, 1024), BF16),
            pltpu.VMEM((4 * OWNERS, STEP), BF16),
            pltpu.VMEM((10, 3, FACES), F32),
            pltpu.SemaphoreType.DMA((FACES // STEP,)),
        ],
        returned, owner, rank, transfer,
        out_specs=[HBM],
    )
    return shell.reshape(4, 3, ROWS, COLS), jnp.transpose(faces, (1, 0, 2))


def solution(mesh):
    placed = (
        P(("grp", "dev"), None),
        P(("grp", "dev")),
        P(None, ("grp", "dev")),
        P(),
        P(("grp", "dev")),
        P(),
        P(),
        P("grp", "dev"),
        P(None, None, "grp", "dev"),
    )
    return jax.shard_map(
        local,
        mesh=mesh,
        in_specs=placed,
        out_specs=(P(None, None, "grp", "dev"), P(None, None, ("grp", "dev"))),
        check_vma=False,
    )
```

```python
import functools

import jax
import jax.numpy as jnp
from jax import lax
from jax.experimental import pallas as pl
from jax.experimental.pallas import tpu as pltpu
from jax.sharding import PartitionSpec as P

SWEEPS = 8
WEIGHT = 2.2
HIGHEST = lax.Precision.HIGHEST
F32 = jnp.float32
BF16 = jnp.bfloat16
I32 = jnp.int32

OWNERS = 128
CAP = 64
COLS = 256
ROWS = 64
PAD_R = 80
PAD_C = 384
FACES = 4096
CHUNK = 256
STEP = 2048
HALF = 32
PLANES = 25
LIMIT = 60
NT = (((1,), (1,)), ((), ()))


def iota(shape, dim):
    return lax.broadcasted_iota(I32, shape, dim)


def dot(a, b):
    return jnp.dot(a, b, preferred_element_type=F32)


def dot_nt(a, b):
    return lax.dot_general(a, b, NT, preferred_element_type=F32)


def exact(a, b):
    return jnp.dot(a, b, precision=HIGHEST, preferred_element_type=F32)


def one_hot(flag):
    return flag.astype(F32).astype(BF16)


def split(x):
    high = x.astype(BF16)
    return high, (x - high.astype(F32)).astype(BF16)


def hot(flag):
    return jnp.where(flag, jnp.ones((), BF16), jnp.zeros((), BF16))


def spread_row(row):
    return jnp.broadcast_to(row, (16, row.shape[1])).astype(BF16)


def hot_rows(row, count):
    wide = spread_row(row)
    step = iota((16, row.shape[1]), 0).astype(F32).astype(BF16)
    return [hot(step == wide - 16.0 * k) for k in range(count // 16)]


def quarters(owner, quarter):
    pieces = hot_rows(owner, OWNERS)
    wide = spread_row(quarter)
    for q in range(4):
        here = hot(wide == q)
        for k, piece in enumerate(pieces):
            yield q * OWNERS + 16 * k, piece * here


def face_kernel(owner_hbm, elem_hbm, state_hbm, scale_hbm, lift_hbm, transfer_hbm, prev_hbm, shell_hbm,
                msg_ref, rank_ref, strip_ref,
                owner_ref, elem_ref, state_ref, scale_ref, lift_ref, transfer_ref, x_ref, hot_ref, acc_ref, sems):
    copies = [
        pltpu.make_async_copy(src, dst, sems.at[i])
        for i, (src, dst) in enumerate((
            (owner_hbm, owner_ref), (transfer_hbm, transfer_ref), (lift_hbm, lift_ref),
            (elem_hbm, elem_ref), (scale_hbm, scale_ref), (state_hbm, state_ref),
            (prev_hbm.at[:, 0:8, :], strip_ref.at[0, 0:12]),
            (prev_hbm.at[:, ROWS - 8:ROWS, :], strip_ref.at[1, 0:12]),
            (shell_hbm.at[0:8, :], strip_ref.at[0, 12]),
            (shell_hbm.at[ROWS - 8:ROWS, :], strip_ref.at[1, 12]),
        ))
    ]
    for copy in copies:
        copy.start()
    x_ref[...] = jnp.zeros_like(x_ref)
    acc_ref[...] = jnp.zeros_like(acc_ref)
    before = iota((CHUNK, 2 * CHUNK), 0)
    upper = iota((CHUNK, 2 * CHUNK), 1)
    upper = one_hot((before < upper) | (upper >= CHUNK))
    copies[0].wait()

    def ranks(i, base):
        part = pl.ds(pl.multiple_of(i * CHUNK, CHUNK), CHUNK)
        mine = (iota((OWNERS, CHUNK), 0) == owner_ref[:, part]).astype(F32)
        counts = dot(mine.astype(BF16), upper)
        rank_ref[:, part] = jnp.sum(mine * (counts[:, :CHUNK] + base), axis=0, keepdims=True)
        return base + counts[:, CHUNK:]

    lax.fori_loop(0, FACES // CHUNK, ranks, jnp.zeros((OWNERS, CHUNK), F32), unroll=True)
    for copy in copies[1:6]:
        copy.wait()
    spread = jnp.concatenate(
        [jnp.pad(transfer_ref[...], ((0, 0), (10 * c, 20 - 10 * c))) for c in range(3)], axis=0
    )
    weights = exact(spread, lift_ref[...].astype(F32))
    high, low = split(weights)

    def body(i, carry):
        part = pl.ds(pl.multiple_of(i * STEP, STEP), STEP)
        rank = rank_ref[:, part].astype(I32)
        for at, piece in quarters(owner_ref[:, part].astype(F32), (rank >> 4).astype(F32)):
            hot_ref[at:at + 16, :] = piece
        place, = hot_rows((rank & 15).astype(F32), 16)
        state = state_ref[:, part]
        load = (dot(high, state) + dot(low, state)) * scale_ref[:, part]
        marker = (elem_ref[:, part] + 1).astype(F32)
        for c in range(13):
            at = 4 * (c % 3) + c // 3
            row = load[at:at + 1] if c < 12 else marker
            top, rest = split(jnp.broadcast_to(row, (16, STEP)))
            x_ref[16 * c:16 * c + 16, :STEP] = place * top
            x_ref[16 * c:16 * c + 16, STEP:] = place * rest
        acc_ref[...] += dot_nt(hot_ref[...], x_ref[:, :STEP]) + dot_nt(hot_ref[...], x_ref[:, STEP:])
        return carry

    lax.fori_loop(0, FACES // STEP, body, 0)
    for q in range(4):
        for t in range(2):
            msg_ref[:, 2 * q + t, :] = acc_ref[q * OWNERS:(q + 1) * OWNERS, 128 * t:128 * t + 128]
    for copy in copies[6:]:
        copy.wait()


def places(marker):
    element = marker.astype(I32) - 1
    row, col = element >> 8, (element & 255).astype(F32)
    pieces = hot_rows(col, COLS)
    wide = spread_row(row.astype(F32))
    low, high = hot(wide < HALF), hot(wide >= HALF)
    columns = [piece * low for piece in pieces] + [piece * high for piece in pieces]
    return (row & (HALF - 1)).astype(F32), columns


def build(turned_ref, mark_ref, q, count, number, a_ref, col_ref):
    for h in range(2):
        markers = mark_ref[pl.ds(pl.multiple_of(16 * q + 8 * h, 8), 8), :]
        for k in range(8):
            lanes = slice(1024 * h + 128 * k, 1024 * h + 128 * k + 128)
            element = markers[k:k + 1].astype(I32) - 1
            for b, piece in enumerate(hot_rows((element & 255).astype(F32), COLS)):
                col_ref[16 * b:16 * b + 16, lanes] = piece
            row_hot = hot_rows(number(element >> 8).astype(F32), count)
            for part in range(2):
                for c in range(12):
                    first = 16 * (c % 8) + 8 * h
                    values = turned_ref[part, 2 * q + c // 8, first:first + 8, :]
                    value = spread_row(values[k:k + 1])
                    at = (12 * part + c) * count
                    for b, piece in enumerate(row_hot):
                        a_ref[at + 16 * b:at + 16 * b + 16, lanes] = piece * value


def edge_scatter_kernel(msg_ref, strip_ref, north_ref, south_ref, turned_ref, mark_ref, a_ref, col_ref, acc_ref):
    north_ref[12:PLANES] = strip_ref[0]
    south_ref[12:PLANES] = strip_ref[1]
    acc_ref[...] = jnp.zeros_like(acc_ref)
    for j in range(8):
        turned = jnp.transpose(msg_ref[:, j, :])
        if j % 2:
            mark_ref[8 * j - 8:8 * j + 8, :] = turned[64:80]
        turned = turned * (1.0 / WEIGHT)
        top = turned.astype(BF16).astype(F32)
        turned_ref[0, j] = top
        turned_ref[1, j] = turned - top

    def body(q, carry):
        build(
            turned_ref, mark_ref, q, 16,
            lambda row: jnp.where(row < 8, row, jnp.where(row >= ROWS - 8, row - (ROWS - 16), -1)), a_ref, col_ref,
        )
        acc_ref[...] += dot_nt(a_ref[...], col_ref[...])
        return carry

    lax.fori_loop(0, 4, body, 0)
    for c in range(12):
        strip = acc_ref[16 * c:16 * c + 16] + acc_ref[192 + 16 * c:208 + 16 * c]
        north_ref[c] = strip[0:8]
        south_ref[c] = strip[8:16]


INNER = ROWS - 16


def scatter_kernel(turned_ref, mark_ref, north_ref, south_ref, load_ref, a_ref, col_ref, acc_ref):
    acc_ref[...] = jnp.zeros_like(acc_ref)

    def body(q, carry):
        build(turned_ref, mark_ref, q, INNER, lambda row: row - 8, a_ref, col_ref)
        acc_ref[...] += dot_nt(a_ref[...], col_ref[...])
        return carry

    lax.fori_loop(0, 4, body, 0)
    for c in range(12):
        load_ref[c, 0:8, :] = north_ref[c]
        load_ref[c, 8:8 + INNER, :] = acc_ref[INNER * c:INNER * c + INNER] + acc_ref[INNER * (12 + c):INNER * (13 + c)]
        load_ref[c, ROWS - 8:ROWS, :] = south_ref[c]


def matrix_kernel(stiff_ref, mat_ref):
    eye = (iota((12, 12), 0) == iota((12, 12), 1)).astype(F32)
    approx = eye / 5.0
    rest = eye - exact(stiff_ref[...], approx)
    for turn in range(8):
        approx = approx + exact(approx, rest)
        if turn < 7:
            rest = exact(rest, rest)
    tall = (iota((96, 12), 0) // 8 == iota((96, 12), 1)).astype(F32)
    wide = (iota((12, 96), 1) // 8 == iota((12, 96), 0)).astype(F32)
    big = exact(exact(tall, approx * WEIGHT), wide)
    big = jnp.where(iota((96, 96), 0) % 8 == iota((96, 96), 1) % 8, big, 0.0)
    high, low = split(big)
    mat_ref[0:96, :] = jnp.concatenate([high, high], axis=1)
    mat_ref[96:192, :] = jnp.concatenate([low, jnp.zeros_like(low)], axis=1)


def columns_kernel(load_ref, prev_ref, scale_ref, south_ref, north_ref, west_ref, east_ref):
    for at, rows, pick in (
        (0, ROWS, lambda p, lanes: scale_ref[:, lanes] if p == 24 else load_ref[p, :, lanes] if p < 12 else prev_ref[p - 12, :, lanes]),
        (ROWS, 8, lambda p, lanes: south_ref[p, :, lanes]),
        (ROWS + 8, 8, lambda p, lanes: north_ref[p, :, lanes]),
    ):
        group = iota((rows, 128), 1) // 8
        for tile in range(2):
            west = jnp.zeros((rows, 128), F32)
            east = jnp.zeros((rows, 128), F32)
            for p in range(16 * tile, min(PLANES, 16 * tile + 16)):
                i = p % 16
                low = pick(p, slice(0, 128))
                high = pick(p, slice(128, 256))
                west = jnp.where(group == i, pltpu.roll(low, 8 * i, 1) if i else low, west)
                east = jnp.where(group == i, pltpu.roll(high, (8 * i + 8) % 128, 1), east)
            west_ref[at:at + rows, 128 * tile:128 * tile + 128] = west
            east_ref[at:at + rows, 128 * tile:128 * tile + 128] = east


def row_ok(shape):
    grp = lax.axis_index("grp")
    row = iota(shape, 0)
    return (row < ROWS) | ((row < ROWS + 8) & (grp < lax.axis_size("grp") - 1)) | ((row >= ROWS + 8) & (grp > 0))


def settle(pad_ref, lanes, ok):
    pad_ref[24, :, lanes] = jnp.where(ok, 1.0 / jnp.where(ok, pad_ref[24, :, lanes], 1.0), 0.0)
    for c in range(12):
        pad_ref[12 + c, :, lanes] = jnp.where(ok, pad_ref[12 + c, :, lanes], 0.0)


def fill_kernel(load_ref, prev_ref, scale_ref, south_ref, north_ref, pad_ref):
    for p in range(PLANES):
        pad_ref[p, 0:ROWS, 0:COLS] = scale_ref[...] if p == 24 else load_ref[p] if p < 12 else prev_ref[p - 12]
        pad_ref[p, ROWS:ROWS + 8, 0:COLS] = south_ref[p]
        pad_ref[p, ROWS + 8:PAD_R, 0:COLS] = north_ref[p]
        pad_ref[p, :, COLS:PAD_C] = jnp.zeros((PAD_R, PAD_C - COLS), F32)
    settle(pad_ref, slice(0, COLS), row_ok((PAD_R, COLS)))


def sweep_kernel(pad_in, from_east_ref, from_west_ref, mat_ref, mark_ref,
                 out_ref, ret_ref, pad_ref, x_ref, hl_ref, turned_ref):
    del pad_in
    lane = iota((PAD_R, 128), 1)
    for p in range(PLANES):
        tile = slice(128 * (p // 16), 128 * (p // 16) + 128)
        low = pltpu.roll(from_east_ref[:, tile], (128 - 8 * (p % 16)) % 128, 1)
        high = pltpu.roll(from_west_ref[:, tile], (248 - 8 * (p % 16)) % 128, 1)
        pad_ref[p, :, COLS:PAD_C] = jnp.where(lane < 8, low, jnp.where(lane >= 120, high, 0.0))
    dev = lax.axis_index("dev")
    ok = row_ok((PAD_R, 128)) & (
        ((lane < 8) & (dev < lax.axis_size("dev") - 1)) | ((lane >= 120) & (dev > 0))
    )
    settle(pad_ref, slice(COLS, PAD_C), ok)
    along = ((1, 1), (0, PAD_C - 1), (3, 1), (2, PAD_C - 1))
    across = ((2, 1), (3, 1), (0, PAD_R - 1), (1, PAD_R - 1))

    def right_side(at):
        n, c = divmod(at, 3)
        return (
            pad_ref[at]
            + pltpu.roll(pad_ref[12 + 3 * along[n][0] + c], along[n][1], 1)
            + pltpu.roll(pad_ref[12 + 3 * across[n][0] + c], across[n][1], 0)
        )

    def sweep(turn, carry):
        for at in range(0, 12, 2):
            first, second = right_side(at), right_side(at + 1)
            for b in range(PAD_R // 8):
                rows = slice(8 * b, 8 * b + 8)
                top, rest = split(jnp.concatenate([first[rows], second[rows]], axis=0))
                lanes = slice(PAD_C * (b % 2), PAD_C * (b % 2) + PAD_C)
                x_ref[b // 2, 8 * at:8 * at + 16, lanes] = top
                x_ref[b // 2, 96 + 8 * at:96 + 8 * at + 16, lanes] = rest
        for b in range(PAD_R // 16):
            solved = dot(mat_ref[...], x_ref[b])
            for h in range(2):
                rows = slice(16 * b + 8 * h, 16 * b + 8 * h + 8)
                lanes = slice(PAD_C * h, PAD_C * h + PAD_C)
                factor = pad_ref[24, rows]
                for at in range(12):
                    pad_ref[12 + at, rows] = (
                        solved[8 * at:8 * at + 8, lanes] + solved[96 + 8 * at:96 + 8 * at + 8, lanes]
                    ) * factor
        return carry

    lax.fori_loop(0, SWEEPS, sweep, 0, unroll=2)
    for c in range(12):
        value = pad_ref[12 + c, 0:ROWS, 0:COLS]
        out_ref[c] = value
        top, rest = split(value)
        for b in range(2):
            part = slice(HALF * b, HALF * (b + 1))
            hl_ref[c * HALF:(c + 1) * HALF, COLS * b:COLS * (b + 1)] = top[part]
            hl_ref[c * HALF:(c + 1) * HALF, 512 + COLS * b:512 + COLS * (b + 1)] = rest[part]

    def gather(q, carry):
        markers = mark_ref[pl.ds(pl.multiple_of(16 * q, 16), 16), :]
        row, columns = places(jnp.concatenate([markers[k:k + 1] for k in range(16)], axis=1))
        columns = jnp.concatenate(columns, axis=0)
        found = dot(hl_ref[:, :512], columns) + dot(hl_ref[:, 512:], columns)
        here = iota((HALF, 2048), 0).astype(F32) == row
        for c in range(12):
            value = jnp.sum(jnp.where(here, found[c * HALF:(c + 1) * HALF], 0.0), axis=0, keepdims=True)
            value = jnp.concatenate([value[:, 128 * k:128 * k + 128] for k in range(16)], axis=0)
            turned_ref[2 * q + c // 8, 16 * (c % 8):16 * (c % 8) + 16, :] = value
        return carry

    lax.fori_loop(0, 4, gather, 0)
    for j in range(8):
        ret_ref[:, j, :] = jnp.transpose(turned_ref[j])


def return_kernel(ret_ref, owner_ref, rank_ref, transfer_ref, out_ref, l_ref, hot_ref, faces_ref, sems):
    for q in range(4):
        for t in range(2):
            count = 128 if t == 0 else 64
            top, rest = split(jnp.transpose(ret_ref[:, 2 * q + t, :])[:count])
            l_ref[128 * t:128 * t + count, 128 * q:128 * q + 128] = top
            l_ref[128 * t:128 * t + count, 512 + 128 * q:512 + 128 * q + 128] = rest
    pick = (iota((80, 10), 0) // 8 == iota((80, 10), 1)).astype(F32)
    spread = lax.dot_general(pick, transfer_ref[...], NT, precision=HIGHEST, preferred_element_type=F32)
    spread = exact(spread, (iota((4, 16), 1) // 3 == iota((4, 16), 0)).astype(F32))
    spread = jnp.where(iota((80, 16), 0) % 8 == iota((80, 16), 1) % 3, spread, 0.0)
    high, low = split(spread)
    copies = []
    for i in range(FACES // STEP):
        part = slice(i * STEP, (i + 1) * STEP)
        rank = rank_ref[:, part].astype(I32)
        for at, piece in quarters(owner_ref[:, part].astype(F32), (rank >> 4).astype(F32)):
            hot_ref[at:at + 16, :] = piece
        found = dot(l_ref[:, :512], hot_ref[...]) + dot(l_ref[:, 512:], hot_ref[...])
        here = iota((16, STEP), 0) == (rank & 15)
        node = jnp.concatenate(
            [jnp.sum(jnp.where(here, found[16 * c:16 * c + 16], 0.0), axis=0, keepdims=True) for c in range(12)]
            + [jnp.zeros((4, STEP), F32)],
            axis=0,
        )
        top, rest = split(node)
        result = dot(high, top) + (dot(high, rest) + dot(low, top))
        for k in range(10):
            faces_ref[k, :, part] = result[8 * k:8 * k + 3]
        copy = pltpu.make_async_copy(faces_ref.at[:, :, part], out_ref.at[:, :, part], sems.at[i])
        copy.start()
        copies.append(copy)
    for copy in copies:
        copy.wait()


VMEM = pl.BlockSpec(memory_space=pltpu.VMEM)
HBM = pl.BlockSpec(memory_space=pl.ANY)


def call(kernel, outs, scratch, *args, hbm=(), out_specs=None, limit=28, alias=None):
    single = not isinstance(outs, (list, tuple))
    shapes = [outs] if single else list(outs)
    result = pl.pallas_call(
        kernel,
        out_shape=shapes,
        in_specs=[HBM if i in hbm else VMEM for i in range(len(args))],
        out_specs=out_specs or [VMEM] * len(shapes),
        scratch_shapes=scratch,
        input_output_aliases=alias or {},
        compiler_params=pltpu.CompilerParams(vmem_limit_bytes=limit * 1024 * 1024),
    )(*args)
    return result[0] if single else result


def arr(*shape, dtype=F32):
    return jax.ShapeDtypeStruct(shape, dtype)


def ring(axis, step):
    count = lax.axis_size(axis)
    return [(i, (i + step) % count) for i in range(count)]


def shift_pair(toward_low, toward_high, axis):
    return lax.ppermute(toward_low, axis, ring(axis, -1)), lax.ppermute(toward_high, axis, ring(axis, 1))


def local(face_owner, face_element, element_state, lift, face_scale, transfer, stiffness_ref, element_scale, displacement_prev):
    owner = face_owner.reshape(1, FACES)
    element = face_element.reshape(1, FACES)
    scale = face_scale.reshape(1, FACES)
    prev = displacement_prev.reshape(12, ROWS, COLS)

    msg, rank, strip = call(
        face_kernel,
        [arr(OWNERS, 8, 128), arr(1, FACES), arr(2, 13, 8, COLS)],
        [
            pltpu.VMEM((1, FACES), I32), pltpu.VMEM((1, FACES), I32), pltpu.VMEM((110, FACES), BF16),
            pltpu.VMEM((1, FACES), F32), pltpu.VMEM((30, 110), BF16), pltpu.VMEM((4, 10), F32),
            pltpu.VMEM((256, 2 * STEP), BF16), pltpu.VMEM((4 * OWNERS, STEP), BF16), pltpu.VMEM((4 * OWNERS, 256), F32),
            pltpu.SemaphoreType.DMA((10,)),
        ],
        owner, element, element_state, scale, lift, transfer, prev, element_scale,
        hbm=(0, 1, 2, 3, 4, 5, 6, 7), limit=LIMIT,
    )
    got = lax.all_to_all(msg, ("grp", "dev"), split_axis=0, concat_axis=0)
    mat = call(matrix_kernel, arr(192, 192, dtype=BF16), [], stiffness_ref)

    north, south, turned, mark = call(
        edge_scatter_kernel,
        [arr(PLANES, 8, COLS), arr(PLANES, 8, COLS), arr(2, 8, 128, 128), arr(64, 128)],
        [
            pltpu.VMEM((24 * 16, 2048), BF16),
            pltpu.VMEM((COLS, 2048), BF16),
            pltpu.VMEM((24 * 16, COLS), F32),
        ],
        got, strip,
    )
    below, above = shift_pair(north, south, "grp")
    load = call(
        scatter_kernel,
        arr(12, ROWS, COLS),
        [
            pltpu.VMEM((24 * INNER, 2048), BF16),
            pltpu.VMEM((COLS, 2048), BF16),
            pltpu.VMEM((24 * INNER, COLS), F32),
        ],
        turned, mark, north, south,
    )
    west, east = call(
        columns_kernel, [arr(PAD_R, 256), arr(PAD_R, 256)], [], load, prev, element_scale, below, above
    )
    from_east, from_west = shift_pair(west, east, "dev")
    pad = call(fill_kernel, arr(PLANES, PAD_R, PAD_C), [], load, prev, element_scale, below, above)

    shell, back, _ = call(
        sweep_kernel,
        [arr(12, ROWS, COLS), arr(OWNERS, 8, 128), arr(PLANES, PAD_R, PAD_C)],
        [
            pltpu.VMEM((PAD_R // 16, 192, 2 * PAD_C), BF16),
            pltpu.VMEM((12 * HALF, 1024), BF16),
            pltpu.VMEM((8, 128, 128), F32),
        ],
        pad, from_east, from_west, mat, mark,
        alias={0: 2},
    )
    returned = lax.all_to_all(back, ("grp", "dev"), split_axis=0, concat_axis=0)
    faces = call(
        return_kernel,
        arr(10, 3, FACES),
        [
            pltpu.VMEM((192, 1024), BF16),
            pltpu.VMEM((4 * OWNERS, STEP), BF16),
            pltpu.VMEM((10, 3, FACES), F32),
            pltpu.SemaphoreType.DMA((FACES // STEP,)),
        ],
        returned, owner, rank, transfer,
        out_specs=[HBM],
    )
    return shell.reshape(4, 3, ROWS, COLS), jnp.transpose(faces, (1, 0, 2))


def solution(mesh):
    placed = (
        P(("grp", "dev"), None),
        P(("grp", "dev")),
        P(None, ("grp", "dev")),
        P(),
        P(("grp", "dev")),
        P(),
        P(),
        P("grp", "dev"),
        P(None, None, "grp", "dev"),
    )
    return jax.shard_map(
        local,
        mesh=mesh,
        in_specs=placed,
        out_specs=(P(None, None, "grp", "dev"), P(None, None, ("grp", "dev"))),
        check_vma=False,
    )
```

```python
import functools

import jax
import jax.numpy as jnp
from jax import lax
from jax.experimental import pallas as pl
from jax.experimental.pallas import tpu as pltpu
from jax.sharding import PartitionSpec as P

SWEEPS = 8
WEIGHT = 2.2
HIGHEST = lax.Precision.HIGHEST
F32 = jnp.float32
BF16 = jnp.bfloat16
I32 = jnp.int32

OWNERS = 128
CAP = 64
COLS = 256
ROWS = 64
PAD_R = 80
PAD_C = 384
FACES = 4096
CHUNK = 256
STEP = 2048
HALF = 32
PLANES = 25
LIMIT = 60
NT = (((1,), (1,)), ((), ()))


def iota(shape, dim):
    return lax.broadcasted_iota(I32, shape, dim)


def dot(a, b):
    return jnp.dot(a, b, preferred_element_type=F32)


def dot_nt(a, b):
    return lax.dot_general(a, b, NT, preferred_element_type=F32)


def exact(a, b):
    return jnp.dot(a, b, precision=HIGHEST, preferred_element_type=F32)


def one_hot(flag):
    return flag.astype(F32).astype(BF16)


def split(x):
    high = x.astype(BF16)
    return high, (x - high.astype(F32)).astype(BF16)


def hot(flag):
    return jnp.where(flag, jnp.ones((), BF16), jnp.zeros((), BF16))


def spread_row(row):
    return jnp.broadcast_to(row, (16, row.shape[1])).astype(BF16)


def hot_rows(row, count):
    wide = spread_row(row)
    step = iota((16, row.shape[1]), 0).astype(F32).astype(BF16)
    return [hot(step == wide - 16.0 * k) for k in range(count // 16)]


def quarters(owner, quarter):
    pieces = hot_rows(owner, OWNERS)
    wide = spread_row(quarter)
    for q in range(4):
        here = hot(wide == q)
        for k, piece in enumerate(pieces):
            yield q * OWNERS + 16 * k, piece * here


def face_kernel(owner_hbm, elem_hbm, state_hbm, scale_hbm, lift_hbm, transfer_hbm, prev_hbm, shell_hbm,
                msg_ref, rank_ref, strip_ref,
                owner_ref, elem_ref, state_ref, scale_ref, lift_ref, transfer_ref, x_ref, hot_ref, acc_ref, sems):
    copies = [
        pltpu.make_async_copy(src, dst, sems.at[i])
        for i, (src, dst) in enumerate((
            (owner_hbm, owner_ref), (transfer_hbm, transfer_ref), (lift_hbm, lift_ref),
            (elem_hbm, elem_ref), (scale_hbm, scale_ref), (state_hbm, state_ref),
            (prev_hbm.at[:, 0:8, :], strip_ref.at[0, 0:12]),
            (prev_hbm.at[:, ROWS - 8:ROWS, :], strip_ref.at[1, 0:12]),
            (shell_hbm.at[0:8, :], strip_ref.at[0, 12]),
            (shell_hbm.at[ROWS - 8:ROWS, :], strip_ref.at[1, 12]),
        ))
    ]
    for copy in copies:
        copy.start()
    x_ref[...] = jnp.zeros_like(x_ref)
    acc_ref[...] = jnp.zeros_like(acc_ref)
    before = iota((CHUNK, 2 * CHUNK), 0)
    upper = iota((CHUNK, 2 * CHUNK), 1)
    upper = one_hot((before < upper) | (upper >= CHUNK))
    copies[0].wait()

    def ranks(i, base):
        part = pl.ds(pl.multiple_of(i * CHUNK, CHUNK), CHUNK)
        mine = (iota((OWNERS, CHUNK), 0) == owner_ref[:, part]).astype(F32)
        counts = dot(mine.astype(BF16), upper)
        rank_ref[:, part] = jnp.sum(mine * (counts[:, :CHUNK] + base), axis=0, keepdims=True)
        return base + counts[:, CHUNK:]

    lax.fori_loop(0, FACES // CHUNK, ranks, jnp.zeros((OWNERS, CHUNK), F32), unroll=True)
    for copy in copies[1:6]:
        copy.wait()
    spread = jnp.concatenate(
        [jnp.pad(transfer_ref[...], ((0, 0), (10 * c, 20 - 10 * c))) for c in range(3)], axis=0
    )
    weights = exact(spread, lift_ref[...].astype(F32))
    high, low = split(weights)

    def body(i, carry):
        part = pl.ds(pl.multiple_of(i * STEP, STEP), STEP)
        rank = rank_ref[:, part].astype(I32)
        for at, piece in quarters(owner_ref[:, part].astype(F32), (rank >> 4).astype(F32)):
            hot_ref[at:at + 16, :] = piece
        place, = hot_rows((rank & 15).astype(F32), 16)
        state = state_ref[:, part]
        load = (dot(high, state) + dot(low, state)) * scale_ref[:, part]
        marker = (elem_ref[:, part] + 1).astype(F32)
        for c in range(13):
            at = 4 * (c % 3) + c // 3
            row = load[at:at + 1] if c < 12 else marker
            top, rest = split(jnp.broadcast_to(row, (16, STEP)))
            x_ref[16 * c:16 * c + 16, :STEP] = place * top
            x_ref[16 * c:16 * c + 16, STEP:] = place * rest
        acc_ref[...] += dot_nt(hot_ref[...], x_ref[:, :STEP]) + dot_nt(hot_ref[...], x_ref[:, STEP:])
        return carry

    lax.fori_loop(0, FACES // STEP, body, 0)
    lane = iota((OWNERS, 128), 1)
    marks = jnp.zeros((OWNERS, 128), F32)
    last = None
    for q in range(4):
        mine = slice(q * OWNERS, (q + 1) * OWNERS)
        msg_ref[:, 0, 128 * q:128 * q + 128] = acc_ref[mine, 0:128]
        late = acc_ref[mine, 128:256]
        marks = jnp.where(lane // 16 == q, pltpu.roll(late, 64 + 16 * q, 1), marks)
        if q % 2:
            at = 512 + 128 * (q // 2)
            msg_ref[:, 0, at:at + 128] = jnp.where(lane < 64, last, pltpu.roll(late, 64, 1))
        last = late
    msg_ref[:, 0, 768:896] = marks
    for copy in copies[6:]:
        copy.wait()


def places(marker):
    element = marker.astype(I32) - 1
    row, col = element >> 8, (element & 255).astype(F32)
    pieces = hot_rows(col, COLS)
    wide = spread_row(row.astype(F32))
    low, high = hot(wide < HALF), hot(wide >= HALF)
    columns = [piece * low for piece in pieces] + [piece * high for piece in pieces]
    return (row & (HALF - 1)).astype(F32), columns


def build(turned_ref, mark_ref, q, count, number, a_ref, col_ref):
    for h in range(2):
        markers = mark_ref[pl.ds(pl.multiple_of(16 * q + 8 * h, 8), 8), :]
        for k in range(8):
            lanes = slice(1024 * h + 128 * k, 1024 * h + 128 * k + 128)
            element = markers[k:k + 1].astype(I32) - 1
            for b, piece in enumerate(hot_rows((element & 255).astype(F32), COLS)):
                col_ref[16 * b:16 * b + 16, lanes] = piece
            row_hot = hot_rows(number(element >> 8).astype(F32), count)
            for part in range(2):
                for c in range(12):
                    first = 16 * (c % 8) + 8 * h
                    values = turned_ref[part, 2 * q + c // 8, first:first + 8, :]
                    value = spread_row(values[k:k + 1])
                    at = (12 * part + c) * count
                    for b, piece in enumerate(row_hot):
                        a_ref[at + 16 * b:at + 16 * b + 16, lanes] = piece * value


def edge_scatter_kernel(msg_ref, strip_ref, north_ref, south_ref, turned_ref, mark_ref, a_ref, col_ref, acc_ref):
    north_ref[12:PLANES] = strip_ref[0]
    south_ref[12:PLANES] = strip_ref[1]
    acc_ref[...] = jnp.zeros_like(acc_ref)
    mark_ref[...] = jnp.transpose(msg_ref[:, 0, 768:896])[:64]
    for j in range(6):
        turned = jnp.transpose(msg_ref[:, 0, 128 * j:128 * j + 128]) * (1.0 / WEIGHT)
        top = turned.astype(BF16).astype(F32)
        for part, value in enumerate((top, turned - top)):
            if j < 4:
                turned_ref[part, 2 * j] = value
            else:
                turned_ref[part, 4 * j - 15, 0:64] = value[0:64]
                turned_ref[part, 4 * j - 13, 0:64] = value[64:128]

    def body(q, carry):
        build(
            turned_ref, mark_ref, q, 16,
            lambda row: jnp.where(row < 8, row, jnp.where(row >= ROWS - 8, row - (ROWS - 16), -1)), a_ref, col_ref,
        )
        acc_ref[...] += dot_nt(a_ref[...], col_ref[...])
        return carry

    lax.fori_loop(0, 4, body, 0)
    for c in range(12):
        strip = acc_ref[16 * c:16 * c + 16] + acc_ref[192 + 16 * c:208 + 16 * c]
        north_ref[c] = strip[0:8]
        south_ref[c] = strip[8:16]


INNER = ROWS - 16


def scatter_kernel(turned_ref, mark_ref, north_ref, south_ref, load_ref, a_ref, col_ref, acc_ref):
    acc_ref[...] = jnp.zeros_like(acc_ref)

    def body(q, carry):
        build(turned_ref, mark_ref, q, INNER, lambda row: row - 8, a_ref, col_ref)
        acc_ref[...] += dot_nt(a_ref[...], col_ref[...])
        return carry

    lax.fori_loop(0, 4, body, 0)
    for c in range(12):
        load_ref[c, 0:8, :] = north_ref[c]
        load_ref[c, 8:8 + INNER, :] = acc_ref[INNER * c:INNER * c + INNER] + acc_ref[INNER * (12 + c):INNER * (13 + c)]
        load_ref[c, ROWS - 8:ROWS, :] = south_ref[c]


def matrix_kernel(stiff_ref, mat_ref):
    eye = (iota((12, 12), 0) == iota((12, 12), 1)).astype(F32)
    approx = eye / 5.0
    rest = eye - exact(stiff_ref[...], approx)
    for turn in range(8):
        approx = approx + exact(approx, rest)
        if turn < 7:
            rest = exact(rest, rest)
    tall = (iota((96, 12), 0) // 8 == iota((96, 12), 1)).astype(F32)
    wide = (iota((12, 96), 1) // 8 == iota((12, 96), 0)).astype(F32)
    big = exact(exact(tall, approx * WEIGHT), wide)
    big = jnp.where(iota((96, 96), 0) % 8 == iota((96, 96), 1) % 8, big, 0.0)
    high, low = split(big)
    mat_ref[0:96, :] = jnp.concatenate([high, high], axis=1)
    mat_ref[96:192, :] = jnp.concatenate([low, jnp.zeros_like(low)], axis=1)


def columns_kernel(load_ref, prev_ref, scale_ref, south_ref, north_ref, west_ref, east_ref):
    for at, rows, pick in (
        (0, ROWS, lambda p, lanes: scale_ref[:, lanes] if p == 24 else load_ref[p, :, lanes] if p < 12 else prev_ref[p - 12, :, lanes]),
        (ROWS, 8, lambda p, lanes: south_ref[p, :, lanes]),
        (ROWS + 8, 8, lambda p, lanes: north_ref[p, :, lanes]),
    ):
        group = iota((rows, 128), 1) // 8
        for tile in range(2):
            west = jnp.zeros((rows, 128), F32)
            east = jnp.zeros((rows, 128), F32)
            for p in range(16 * tile, min(PLANES, 16 * tile + 16)):
                i = p % 16
                low = pick(p, slice(0, 128))
                high = pick(p, slice(128, 256))
                west = jnp.where(group == i, pltpu.roll(low, 8 * i, 1) if i else low, west)
                east = jnp.where(group == i, pltpu.roll(high, (8 * i + 8) % 128, 1), east)
            west_ref[at:at + rows, 128 * tile:128 * tile + 128] = west
            east_ref[at:at + rows, 128 * tile:128 * tile + 128] = east


def row_ok(shape):
    grp = lax.axis_index("grp")
    row = iota(shape, 0)
    return (row < ROWS) | ((row < ROWS + 8) & (grp < lax.axis_size("grp") - 1)) | ((row >= ROWS + 8) & (grp > 0))


def settle(pad_ref, lanes, ok):
    pad_ref[24, :, lanes] = jnp.where(ok, 1.0 / jnp.where(ok, pad_ref[24, :, lanes], 1.0), 0.0)
    for c in range(12):
        pad_ref[12 + c, :, lanes] = jnp.where(ok, pad_ref[12 + c, :, lanes], 0.0)


def fill_kernel(load_ref, prev_ref, scale_ref, south_ref, north_ref, pad_ref):
    for p in range(PLANES):
        pad_ref[p, 0:ROWS, 0:COLS] = scale_ref[...] if p == 24 else load_ref[p] if p < 12 else prev_ref[p - 12]
        pad_ref[p, ROWS:ROWS + 8, 0:COLS] = south_ref[p]
        pad_ref[p, ROWS + 8:PAD_R, 0:COLS] = north_ref[p]
        pad_ref[p, :, COLS:PAD_C] = jnp.zeros((PAD_R, PAD_C - COLS), F32)
    settle(pad_ref, slice(0, COLS), row_ok((PAD_R, COLS)))


def sweep_kernel(pad_in, from_east_ref, from_west_ref, mat_ref, mark_ref,
                 out_ref, ret_ref, pad_ref, x_ref, hl_ref, turned_ref):
    del pad_in
    lane = iota((PAD_R, 128), 1)
    for p in range(PLANES):
        tile = slice(128 * (p // 16), 128 * (p // 16) + 128)
        low = pltpu.roll(from_east_ref[:, tile], (128 - 8 * (p % 16)) % 128, 1)
        high = pltpu.roll(from_west_ref[:, tile], (248 - 8 * (p % 16)) % 128, 1)
        pad_ref[p, :, COLS:PAD_C] = jnp.where(lane < 8, low, jnp.where(lane >= 120, high, 0.0))
    dev = lax.axis_index("dev")
    ok = row_ok((PAD_R, 128)) & (
        ((lane < 8) & (dev < lax.axis_size("dev") - 1)) | ((lane >= 120) & (dev > 0))
    )
    settle(pad_ref, slice(COLS, PAD_C), ok)
    along = ((1, 1), (0, PAD_C - 1), (3, 1), (2, PAD_C - 1))
    across = ((2, 1), (3, 1), (0, PAD_R - 1), (1, PAD_R - 1))

    def right_side(at):
        n, c = divmod(at, 3)
        return (
            pad_ref[at]
            + pltpu.roll(pad_ref[12 + 3 * along[n][0] + c], along[n][1], 1)
            + pltpu.roll(pad_ref[12 + 3 * across[n][0] + c], across[n][1], 0)
        )

    def sweep(turn, carry):
        for at in range(0, 12, 2):
            first, second = right_side(at), right_side(at + 1)
            for b in range(PAD_R // 8):
                rows = slice(8 * b, 8 * b + 8)
                top, rest = split(jnp.concatenate([first[rows], second[rows]], axis=0))
                lanes = slice(PAD_C * (b % 2), PAD_C * (b % 2) + PAD_C)
                x_ref[b // 2, 8 * at:8 * at + 16, lanes] = top
                x_ref[b // 2, 96 + 8 * at:96 + 8 * at + 16, lanes] = rest
        for b in range(PAD_R // 16):
            solved = dot(mat_ref[...], x_ref[b])
            for h in range(2):
                rows = slice(16 * b + 8 * h, 16 * b + 8 * h + 8)
                lanes = slice(PAD_C * h, PAD_C * h + PAD_C)
                factor = pad_ref[24, rows]
                for at in range(12):
                    pad_ref[12 + at, rows] = (
                        solved[8 * at:8 * at + 8, lanes] + solved[96 + 8 * at:96 + 8 * at + 8, lanes]
                    ) * factor
        return carry

    lax.fori_loop(0, SWEEPS, sweep, 0, unroll=2)
    for c in range(12):
        value = pad_ref[12 + c, 0:ROWS, 0:COLS]
        out_ref[c] = value
        top, rest = split(value)
        for b in range(2):
            part = slice(HALF * b, HALF * (b + 1))
            hl_ref[c * HALF:(c + 1) * HALF, COLS * b:COLS * (b + 1)] = top[part]
            hl_ref[c * HALF:(c + 1) * HALF, 512 + COLS * b:512 + COLS * (b + 1)] = rest[part]

    def gather(q, carry):
        markers = mark_ref[pl.ds(pl.multiple_of(16 * q, 16), 16), :]
        row, columns = places(jnp.concatenate([markers[k:k + 1] for k in range(16)], axis=1))
        columns = jnp.concatenate(columns, axis=0)
        found = dot(hl_ref[:, :512], columns) + dot(hl_ref[:, 512:], columns)
        here = iota((HALF, 2048), 0).astype(F32) == row
        for c in range(12):
            value = jnp.sum(jnp.where(here, found[c * HALF:(c + 1) * HALF], 0.0), axis=0, keepdims=True)
            value = jnp.concatenate([value[:, 128 * k:128 * k + 128] for k in range(16)], axis=0)
            turned_ref[2 * q + c // 8, 16 * (c % 8):16 * (c % 8) + 16, :] = value
        return carry

    lax.fori_loop(0, 4, gather, 0)
    for q in range(4):
        ret_ref[:, 0, 128 * q:128 * q + 128] = jnp.transpose(turned_ref[2 * q])
    for j in range(2):
        late = jnp.concatenate([turned_ref[4 * j + 1, 0:64], turned_ref[4 * j + 3, 0:64]], axis=0)
        ret_ref[:, 0, 512 + 128 * j:640 + 128 * j] = jnp.transpose(late)


def return_kernel(ret_ref, owner_ref, rank_ref, transfer_ref, out_ref, l_ref, hot_ref, faces_ref, sems):
    for j in range(6):
        top, rest = split(jnp.transpose(ret_ref[:, 0, 128 * j:128 * j + 128]))
        for part, value in enumerate((top, rest)):
            if j < 4:
                at = 512 * part + 128 * j
                l_ref[0:128, at:at + 128] = value
            else:
                at = 512 * part + 256 * (j - 4)
                l_ref[128:192, at:at + 128] = value[0:64]
                l_ref[128:192, at + 128:at + 256] = value[64:128]
    pick = (iota((80, 10), 0) // 8 == iota((80, 10), 1)).astype(F32)
    spread = lax.dot_general(pick, transfer_ref[...], NT, precision=HIGHEST, preferred_element_type=F32)
    spread = exact(spread, (iota((4, 16), 1) // 3 == iota((4, 16), 0)).astype(F32))
    spread = jnp.where(iota((80, 16), 0) % 8 == iota((80, 16), 1) % 3, spread, 0.0)
    high, low = split(spread)
    copies = []
    for i in range(FACES // STEP):
        part = slice(i * STEP, (i + 1) * STEP)
        rank = rank_ref[:, part].astype(I32)
        for at, piece in quarters(owner_ref[:, part].astype(F32), (rank >> 4).astype(F32)):
            hot_ref[at:at + 16, :] = piece
        found = dot(l_ref[:, :512], hot_ref[...]) + dot(l_ref[:, 512:], hot_ref[...])
        here = iota((16, STEP), 0) == (rank & 15)
        node = jnp.concatenate(
            [jnp.sum(jnp.where(here, found[16 * c:16 * c + 16], 0.0), axis=0, keepdims=True) for c in range(12)]
            + [jnp.zeros((4, STEP), F32)],
            axis=0,
        )
        top, rest = split(node)
        result = dot(high, top) + (dot(high, rest) + dot(low, top))
        for k in range(10):
            faces_ref[k, :, part] = result[8 * k:8 * k + 3]
        copy = pltpu.make_async_copy(faces_ref.at[:, :, part], out_ref.at[:, :, part], sems.at[i])
        copy.start()
        copies.append(copy)
    for copy in copies:
        copy.wait()


VMEM = pl.BlockSpec(memory_space=pltpu.VMEM)
HBM = pl.BlockSpec(memory_space=pl.ANY)


def call(kernel, outs, scratch, *args, hbm=(), out_specs=None, limit=28, alias=None):
    single = not isinstance(outs, (list, tuple))
    shapes = [outs] if single else list(outs)
    result = pl.pallas_call(
        kernel,
        out_shape=shapes,
        in_specs=[HBM if i in hbm else VMEM for i in range(len(args))],
        out_specs=out_specs or [VMEM] * len(shapes),
        scratch_shapes=scratch,
        input_output_aliases=alias or {},
        compiler_params=pltpu.CompilerParams(vmem_limit_bytes=limit * 1024 * 1024),
    )(*args)
    return result[0] if single else result


def arr(*shape, dtype=F32):
    return jax.ShapeDtypeStruct(shape, dtype)


def ring(axis, step):
    count = lax.axis_size(axis)
    return [(i, (i + step) % count) for i in range(count)]


def shift_pair(toward_low, toward_high, axis):
    return lax.ppermute(toward_low, axis, ring(axis, -1)), lax.ppermute(toward_high, axis, ring(axis, 1))


def local(face_owner, face_element, element_state, lift, face_scale, transfer, stiffness_ref, element_scale, displacement_prev):
    owner = face_owner.reshape(1, FACES)
    element = face_element.reshape(1, FACES)
    scale = face_scale.reshape(1, FACES)
    prev = displacement_prev.reshape(12, ROWS, COLS)

    msg, rank, strip = call(
        face_kernel,
        [arr(OWNERS, 1, 896), arr(1, FACES), arr(2, 13, 8, COLS)],
        [
            pltpu.VMEM((1, FACES), I32), pltpu.VMEM((1, FACES), I32), pltpu.VMEM((110, FACES), BF16),
            pltpu.VMEM((1, FACES), F32), pltpu.VMEM((30, 110), BF16), pltpu.VMEM((4, 10), F32),
            pltpu.VMEM((256, 2 * STEP), BF16), pltpu.VMEM((4 * OWNERS, STEP), BF16), pltpu.VMEM((4 * OWNERS, 256), F32),
            pltpu.SemaphoreType.DMA((10,)),
        ],
        owner, element, element_state, scale, lift, transfer, prev, element_scale,
        hbm=(0, 1, 2, 3, 4, 5, 6, 7), limit=LIMIT,
    )
    got = lax.all_to_all(msg, ("grp", "dev"), split_axis=0, concat_axis=0)
    mat = call(matrix_kernel, arr(192, 192, dtype=BF16), [], stiffness_ref)

    north, south, turned, mark = call(
        edge_scatter_kernel,
        [arr(PLANES, 8, COLS), arr(PLANES, 8, COLS), arr(2, 8, 128, 128), arr(64, 128)],
        [
            pltpu.VMEM((24 * 16, 2048), BF16),
            pltpu.VMEM((COLS, 2048), BF16),
            pltpu.VMEM((24 * 16, COLS), F32),
        ],
        got, strip,
    )
    below, above = shift_pair(north, south, "grp")
    load = call(
        scatter_kernel,
        arr(12, ROWS, COLS),
        [
            pltpu.VMEM((24 * INNER, 2048), BF16),
            pltpu.VMEM((COLS, 2048), BF16),
            pltpu.VMEM((24 * INNER, COLS), F32),
        ],
        turned, mark, north, south,
    )
    west, east = call(
        columns_kernel, [arr(PAD_R, 256), arr(PAD_R, 256)], [], load, prev, element_scale, below, above
    )
    from_east, from_west = shift_pair(west, east, "dev")
    pad = call(fill_kernel, arr(PLANES, PAD_R, PAD_C), [], load, prev, element_scale, below, above)

    shell, back, _ = call(
        sweep_kernel,
        [arr(12, ROWS, COLS), arr(OWNERS, 1, 768), arr(PLANES, PAD_R, PAD_C)],
        [
            pltpu.VMEM((PAD_R // 16, 192, 2 * PAD_C), BF16),
            pltpu.VMEM((12 * HALF, 1024), BF16),
            pltpu.VMEM((8, 128, 128), F32),
        ],
        pad, from_east, from_west, mat, mark,
        alias={0: 2},
    )
    returned = lax.all_to_all(back, ("grp", "dev"), split_axis=0, concat_axis=0)
    faces = call(
        return_kernel,
        arr(10, 3, FACES),
        [
            pltpu.VMEM((192, 1024), BF16),
            pltpu.VMEM((4 * OWNERS, STEP), BF16),
            pltpu.VMEM((10, 3, FACES), F32),
            pltpu.SemaphoreType.DMA((FACES // STEP,)),
        ],
        returned, owner, rank, transfer,
        out_specs=[HBM],
    )
    return shell.reshape(4, 3, ROWS, COLS), jnp.transpose(faces, (1, 0, 2))


def solution(mesh):
    placed = (
        P(("grp", "dev"), None),
        P(("grp", "dev")),
        P(None, ("grp", "dev")),
        P(),
        P(("grp", "dev")),
        P(),
        P(),
        P("grp", "dev"),
        P(None, None, "grp", "dev"),
    )
    return jax.shard_map(
        local,
        mesh=mesh,
        in_specs=placed,
        out_specs=(P(None, None, "grp", "dev"), P(None, None, ("grp", "dev"))),
        check_vma=False,
    )
```

```python
import functools

import jax
import jax.numpy as jnp
from jax import lax
from jax.experimental import pallas as pl
from jax.experimental.pallas import tpu as pltpu
from jax.sharding import PartitionSpec as P

SWEEPS = 8
WEIGHT = 2.2
HIGHEST = lax.Precision.HIGHEST
F32 = jnp.float32
BF16 = jnp.bfloat16
I32 = jnp.int32

OWNERS = 128
CAP = 64
COLS = 256
ROWS = 64
PAD_R = 80
PAD_C = 384
FACES = 4096
CHUNK = 256
STEP = 2048
HALF = 32
PLANES = 25
STRIP = 4096
LIMIT = 60
NT = (((1,), (1,)), ((), ()))


def iota(shape, dim):
    return lax.broadcasted_iota(I32, shape, dim)


def dot(a, b):
    return jnp.dot(a, b, preferred_element_type=F32)


def dot_nt(a, b):
    return lax.dot_general(a, b, NT, preferred_element_type=F32)


def exact(a, b):
    return jnp.dot(a, b, precision=HIGHEST, preferred_element_type=F32)


def one_hot(flag):
    return flag.astype(F32).astype(BF16)


def split(x):
    high = x.astype(BF16)
    return high, (x - high.astype(F32)).astype(BF16)


def hot(flag):
    return jnp.where(flag, jnp.ones((), BF16), jnp.zeros((), BF16))


def spread_row(row):
    return jnp.broadcast_to(row, (16, row.shape[1])).astype(BF16)


def hot_rows(row, count):
    wide = spread_row(row)
    step = iota((16, row.shape[1]), 0).astype(F32).astype(BF16)
    return [hot(step == wide - 16.0 * k) for k in range(count // 16)]


def quarters(owner, quarter):
    pieces = hot_rows(owner, OWNERS)
    wide = spread_row(quarter)
    for q in range(4):
        here = hot(wide == q)
        for k, piece in enumerate(pieces):
            yield q * OWNERS + 16 * k, piece * here


def face_kernel(owner_hbm, elem_hbm, state_hbm, scale_hbm, lift_hbm, transfer_hbm, prev_hbm, shell_hbm,
                msg_ref, rank_ref, strip_ref,
                owner_ref, elem_ref, state_ref, scale_ref, lift_ref, transfer_ref, stage_ref, x_ref, hot_ref, acc_ref,
                sems):
    copies = [
        pltpu.make_async_copy(src, dst, sems.at[i])
        for i, (src, dst) in enumerate((
            (owner_hbm, owner_ref), (transfer_hbm, transfer_ref), (lift_hbm, lift_ref),
            (elem_hbm, elem_ref), (scale_hbm, scale_ref), (state_hbm, state_ref),
            (prev_hbm.at[:, 0:8, :], stage_ref.at[0, 0:12]),
            (prev_hbm.at[:, ROWS - 8:ROWS, :], stage_ref.at[1, 0:12]),
            (shell_hbm.at[0:8, :], stage_ref.at[0, 12]),
            (shell_hbm.at[ROWS - 8:ROWS, :], stage_ref.at[1, 12]),
        ))
    ]
    for copy in copies:
        copy.start()
    x_ref[...] = jnp.zeros_like(x_ref)
    acc_ref[...] = jnp.zeros_like(acc_ref)
    before = iota((CHUNK, 2 * CHUNK), 0)
    upper = iota((CHUNK, 2 * CHUNK), 1)
    upper = one_hot((before < upper) | (upper >= CHUNK))
    copies[0].wait()

    def ranks(i, base):
        part = pl.ds(pl.multiple_of(i * CHUNK, CHUNK), CHUNK)
        mine = (iota((OWNERS, CHUNK), 0) == owner_ref[:, part]).astype(F32)
        counts = dot(mine.astype(BF16), upper)
        rank_ref[:, part] = jnp.sum(mine * (counts[:, :CHUNK] + base), axis=0, keepdims=True)
        return base + counts[:, CHUNK:]

    lax.fori_loop(0, FACES // CHUNK, ranks, jnp.zeros((OWNERS, CHUNK), F32), unroll=True)
    for copy in copies[1:]:
        copy.wait()
    keeps = [pltpu.make_async_copy(stage_ref.at[i], strip_ref.at[i, 0:13], sems.at[10 + i]) for i in range(2)]
    for copy in keeps:
        copy.start()
    spread = jnp.concatenate(
        [jnp.pad(transfer_ref[...], ((0, 0), (10 * c, 20 - 10 * c))) for c in range(3)], axis=0
    )
    weights = exact(spread, lift_ref[...].astype(F32))
    high, low = split(weights)

    def body(i, carry):
        part = pl.ds(pl.multiple_of(i * STEP, STEP), STEP)
        rank = rank_ref[:, part].astype(I32)
        for at, piece in quarters(owner_ref[:, part].astype(F32), (rank >> 4).astype(F32)):
            hot_ref[at:at + 16, :] = piece
        place, = hot_rows((rank & 15).astype(F32), 16)
        state = state_ref[:, part]
        load = (dot(high, state) + dot(low, state)) * scale_ref[:, part]
        marker = (elem_ref[:, part] + 1).astype(F32)
        for c in range(13):
            at = 4 * (c % 3) + c // 3
            row = load[at:at + 1] if c < 12 else marker
            top, rest = split(jnp.broadcast_to(row, (16, STEP)))
            x_ref[16 * c:16 * c + 16, :STEP] = place * top
            x_ref[16 * c:16 * c + 16, STEP:] = place * rest
        acc_ref[...] += dot_nt(hot_ref[...], x_ref[:, :STEP]) + dot_nt(hot_ref[...], x_ref[:, STEP:])
        return carry

    lax.fori_loop(0, FACES // STEP, body, 0)
    lane = iota((OWNERS, 128), 1)
    marks = jnp.zeros((OWNERS, 128), F32)
    last = None
    for q in range(4):
        mine = slice(q * OWNERS, (q + 1) * OWNERS)
        msg_ref[:, 0, 128 * q:128 * q + 128] = acc_ref[mine, 0:128]
        late = acc_ref[mine, 128:256]
        marks = jnp.where(lane // 16 == q, pltpu.roll(late, 64 + 16 * q, 1), marks)
        if q % 2:
            at = 512 + 128 * (q // 2)
            msg_ref[:, 0, at:at + 128] = jnp.where(lane < 64, last, pltpu.roll(late, 64, 1))
        last = late
    msg_ref[:, 0, 768:896] = marks
    for copy in keeps:
        copy.wait()


def places(marker):
    element = marker.astype(I32) - 1
    row, col = element >> 8, (element & 255).astype(F32)
    pieces = hot_rows(col, COLS)
    wide = spread_row(row.astype(F32))
    low, high = hot(wide < HALF), hot(wide >= HALF)
    columns = [piece * low for piece in pieces] + [piece * high for piece in pieces]
    return (row & (HALF - 1)).astype(F32), columns


def build(turned_ref, mark_ref, q, count, number, a_ref, col_ref):
    for h in range(2):
        markers = mark_ref[pl.ds(pl.multiple_of(16 * q + 8 * h, 8), 8), :]
        for k in range(8):
            lanes = slice(1024 * h + 128 * k, 1024 * h + 128 * k + 128)
            element = markers[k:k + 1].astype(I32) - 1
            for b, piece in enumerate(hot_rows((element & 255).astype(F32), COLS)):
                col_ref[16 * b:16 * b + 16, lanes] = piece
            row_hot = hot_rows(number(element >> 8).astype(F32), count)
            for part in range(2):
                for c in range(12):
                    first = 16 * (c % 8) + 8 * h
                    values = turned_ref[part, 2 * q + c // 8, first:first + 8, :]
                    value = spread_row(values[k:k + 1])
                    at = (12 * part + c) * count
                    for b, piece in enumerate(row_hot):
                        a_ref[at + 16 * b:at + 16 * b + 16, lanes] = piece * value


def edge_scatter_kernel(msg_ref, strip_ref, north_ref, south_ref, turned_ref, mark_ref,
                        a_ref, col_ref, acc_ref, sems):
    copies = [
        pltpu.make_async_copy(strip_ref.at[i, 0:13], ref.at[12:PLANES], sems.at[i])
        for i, ref in enumerate((north_ref, south_ref))
    ]
    for copy in copies:
        copy.start()
    acc_ref[...] = jnp.zeros_like(acc_ref)
    mark_ref[...] = jnp.transpose(msg_ref[:, 0, 768:896])[:64]
    for j in range(6):
        turned = jnp.transpose(msg_ref[:, 0, 128 * j:128 * j + 128]) * (1.0 / WEIGHT)
        top = turned.astype(BF16).astype(F32)
        for part, value in enumerate((top, turned - top)):
            if j < 4:
                turned_ref[part, 2 * j] = value
            else:
                turned_ref[part, 4 * j - 15, 0:64] = value[0:64]
                turned_ref[part, 4 * j - 13, 0:64] = value[64:128]

    def body(q, carry):
        build(
            turned_ref, mark_ref, q, 16,
            lambda row: jnp.where(row < 8, row, jnp.where(row >= ROWS - 8, row - (ROWS - 16), -1)), a_ref, col_ref,
        )
        acc_ref[...] += dot_nt(a_ref[...], col_ref[...])
        return carry

    lax.fori_loop(0, 4, body, 0)
    for c in range(12):
        strip = acc_ref[16 * c:16 * c + 16] + acc_ref[192 + 16 * c:208 + 16 * c]
        north_ref[c] = strip[0:8]
        south_ref[c] = strip[8:16]
    for copy in copies:
        copy.wait()


INNER = ROWS - 16


def scatter_kernel(turned_ref, mark_ref, north_ref, south_ref, load_ref, a_ref, col_ref, acc_ref):
    acc_ref[...] = jnp.zeros_like(acc_ref)

    def body(q, carry):
        build(turned_ref, mark_ref, q, INNER, lambda row: row - 8, a_ref, col_ref)
        acc_ref[...] += dot_nt(a_ref[...], col_ref[...])
        return carry

    lax.fori_loop(0, 4, body, 0)
    for c in range(12):
        load_ref[c, 0:8, :] = north_ref[c]
        load_ref[c, 8:8 + INNER, :] = acc_ref[INNER * c:INNER * c + INNER] + acc_ref[INNER * (12 + c):INNER * (13 + c)]
        load_ref[c, ROWS - 8:ROWS, :] = south_ref[c]


def matrix_kernel(stiff_ref, mat_ref):
    eye = (iota((12, 12), 0) == iota((12, 12), 1)).astype(F32)
    approx = eye / 5.0
    rest = eye - exact(stiff_ref[...], approx)
    for turn in range(8):
        approx = approx + exact(approx, rest)
        if turn < 7:
            rest = exact(rest, rest)
    tall = (iota((96, 12), 0) // 8 == iota((96, 12), 1)).astype(F32)
    wide = (iota((12, 96), 1) // 8 == iota((12, 96), 0)).astype(F32)
    big = exact(exact(tall, approx * WEIGHT), wide)
    big = jnp.where(iota((96, 96), 0) % 8 == iota((96, 96), 1) % 8, big, 0.0)
    high, low = split(big)
    mat_ref[0:96, :] = jnp.concatenate([high, high], axis=1)
    mat_ref[96:192, :] = jnp.concatenate([low, jnp.zeros_like(low)], axis=1)


def columns_kernel(load_ref, prev_ref, scale_ref, south_ref, north_ref, west_ref, east_ref):
    for at, rows, pick in (
        (0, ROWS, lambda p, lanes: scale_ref[:, lanes] if p == 24 else load_ref[p, :, lanes] if p < 12 else prev_ref[p - 12, :, lanes]),
        (ROWS, 8, lambda p, lanes: south_ref[p, :, lanes]),
        (ROWS + 8, 8, lambda p, lanes: north_ref[p, :, lanes]),
    ):
        group = iota((rows, 128), 1) // 8
        for tile in range(2):
            west = jnp.zeros((rows, 128), F32)
            east = jnp.zeros((rows, 128), F32)
            for p in range(16 * tile, min(PLANES, 16 * tile + 16)):
                i = p % 16
                low = pick(p, slice(0, 128))
                high = pick(p, slice(128, 256))
                west = jnp.where(group == i, pltpu.roll(low, 8 * i, 1) if i else low, west)
                east = jnp.where(group == i, pltpu.roll(high, (8 * i + 8) % 128, 1), east)
            west_ref[at:at + rows, 128 * tile:128 * tile + 128] = west
            east_ref[at:at + rows, 128 * tile:128 * tile + 128] = east


def row_ok(shape):
    grp = lax.axis_index("grp")
    row = iota(shape, 0)
    return (row < ROWS) | ((row < ROWS + 8) & (grp < lax.axis_size("grp") - 1)) | ((row >= ROWS + 8) & (grp > 0))


def settle(pad_ref, lanes, ok):
    pad_ref[24, :, lanes] = jnp.where(ok, 1.0 / jnp.where(ok, pad_ref[24, :, lanes], 1.0), 0.0)
    for c in range(12):
        pad_ref[12 + c, :, lanes] = jnp.where(ok, pad_ref[12 + c, :, lanes], 0.0)


def fill_kernel(load_ref, prev_ref, scale_ref, south_ref, north_ref, pad_ref):
    for p in range(PLANES):
        pad_ref[p, 0:ROWS, 0:COLS] = scale_ref[...] if p == 24 else load_ref[p] if p < 12 else prev_ref[p - 12]
        pad_ref[p, ROWS:ROWS + 8, 0:COLS] = south_ref[p]
        pad_ref[p, ROWS + 8:PAD_R, 0:COLS] = north_ref[p]
        pad_ref[p, :, COLS:PAD_C] = jnp.zeros((PAD_R, PAD_C - COLS), F32)
    settle(pad_ref, slice(0, COLS), row_ok((PAD_R, COLS)))


def sweep_kernel(pad_in, from_east_ref, from_west_ref, mat_ref, mark_ref,
                 out_ref, ret_ref, pad_ref, x_ref, hl_ref, turned_ref):
    del pad_in
    lane = iota((PAD_R, 128), 1)
    for p in range(PLANES):
        tile = slice(128 * (p // 16), 128 * (p // 16) + 128)
        low = pltpu.roll(from_east_ref[:, tile], (128 - 8 * (p % 16)) % 128, 1)
        high = pltpu.roll(from_west_ref[:, tile], (248 - 8 * (p % 16)) % 128, 1)
        pad_ref[p, :, COLS:PAD_C] = jnp.where(lane < 8, low, jnp.where(lane >= 120, high, 0.0))
    dev = lax.axis_index("dev")
    ok = row_ok((PAD_R, 128)) & (
        ((lane < 8) & (dev < lax.axis_size("dev") - 1)) | ((lane >= 120) & (dev > 0))
    )
    settle(pad_ref, slice(COLS, PAD_C), ok)
    along = ((1, 1), (0, PAD_C - 1), (3, 1), (2, PAD_C - 1))
    across = ((2, 1), (3, 1), (0, PAD_R - 1), (1, PAD_R - 1))

    def right_side(at):
        n, c = divmod(at, 3)
        return (
            pad_ref[at]
            + pltpu.roll(pad_ref[12 + 3 * along[n][0] + c], along[n][1], 1)
            + pltpu.roll(pad_ref[12 + 3 * across[n][0] + c], across[n][1], 0)
        )

    def sweep(turn, carry):
        for at in range(0, 12, 2):
            first, second = right_side(at), right_side(at + 1)
            for b in range(PAD_R // 8):
                rows = slice(8 * b, 8 * b + 8)
                top, rest = split(jnp.concatenate([first[rows], second[rows]], axis=0))
                lanes = slice(PAD_C * (b % 2), PAD_C * (b % 2) + PAD_C)
                x_ref[b // 2, 8 * at:8 * at + 16, lanes] = top
                x_ref[b // 2, 96 + 8 * at:96 + 8 * at + 16, lanes] = rest
        for b in range(PAD_R // 16):
            solved = dot(mat_ref[...], x_ref[b])
            for h in range(2):
                rows = slice(16 * b + 8 * h, 16 * b + 8 * h + 8)
                lanes = slice(PAD_C * h, PAD_C * h + PAD_C)
                factor = pad_ref[24, rows]
                for at in range(12):
                    pad_ref[12 + at, rows] = (
                        solved[8 * at:8 * at + 8, lanes] + solved[96 + 8 * at:96 + 8 * at + 8, lanes]
                    ) * factor
        return carry

    lax.fori_loop(0, SWEEPS, sweep, 0, unroll=2)
    for c in range(12):
        value = pad_ref[12 + c, 0:ROWS, 0:COLS]
        out_ref[c] = value
        top, rest = split(value)
        for b in range(2):
            part = slice(HALF * b, HALF * (b + 1))
            hl_ref[c * HALF:(c + 1) * HALF, COLS * b:COLS * (b + 1)] = top[part]
            hl_ref[c * HALF:(c + 1) * HALF, 512 + COLS * b:512 + COLS * (b + 1)] = rest[part]

    def gather(q, carry):
        markers = mark_ref[pl.ds(pl.multiple_of(16 * q, 16), 16), :]
        row, columns = places(jnp.concatenate([markers[k:k + 1] for k in range(16)], axis=1))
        columns = jnp.concatenate(columns, axis=0)
        found = dot(hl_ref[:, :512], columns) + dot(hl_ref[:, 512:], columns)
        here = iota((HALF, 2048), 0).astype(F32) == row
        for c in range(12):
            value = jnp.sum(jnp.where(here, found[c * HALF:(c + 1) * HALF], 0.0), axis=0, keepdims=True)
            value = jnp.concatenate([value[:, 128 * k:128 * k + 128] for k in range(16)], axis=0)
            turned_ref[2 * q + c // 8, 16 * (c % 8):16 * (c % 8) + 16, :] = value
        return carry

    lax.fori_loop(0, 4, gather, 0)
    for q in range(4):
        ret_ref[:, 0, 128 * q:128 * q + 128] = jnp.transpose(turned_ref[2 * q])
    for j in range(2):
        late = jnp.concatenate([turned_ref[4 * j + 1, 0:64], turned_ref[4 * j + 3, 0:64]], axis=0)
        ret_ref[:, 0, 512 + 128 * j:640 + 128 * j] = jnp.transpose(late)


def return_kernel(ret_ref, owner_ref, rank_ref, transfer_ref, out_ref, l_ref, hot_ref, faces_ref, sems):
    for j in range(6):
        top, rest = split(jnp.transpose(ret_ref[:, 0, 128 * j:128 * j + 128]))
        for part, value in enumerate((top, rest)):
            at = 192 * part
            if j < 4:
                l_ref[at:at + 128, 128 * j:128 * j + 128] = value
            else:
                lane = 256 * (j - 4)
                l_ref[at + 128:at + 192, lane:lane + 128] = value[0:64]
                l_ref[at + 128:at + 192, lane + 128:lane + 256] = value[64:128]
    pick = (iota((80, 10), 0) // 8 == iota((80, 10), 1)).astype(F32)
    spread = lax.dot_general(pick, transfer_ref[...], NT, precision=HIGHEST, preferred_element_type=F32)
    spread = exact(spread, (iota((4, 16), 1) // 3 == iota((4, 16), 0)).astype(F32))
    spread = jnp.where(iota((80, 16), 0) % 8 == iota((80, 16), 1) % 3, spread, 0.0)
    high, low = split(spread)
    copies = []
    for i in range(FACES // STEP):
        part = slice(i * STEP, (i + 1) * STEP)
        rank = rank_ref[:, part].astype(I32)
        for at, piece in quarters(owner_ref[:, part].astype(F32), (rank >> 4).astype(F32)):
            hot_ref[at:at + 16, :] = piece
        found = dot(l_ref[...], hot_ref[...])
        found = found[:192] + found[192:]
        here = iota((16, STEP), 0) == (rank & 15)
        node = jnp.concatenate(
            [jnp.sum(jnp.where(here, found[16 * c:16 * c + 16], 0.0), axis=0, keepdims=True) for c in range(12)]
            + [jnp.zeros((4, STEP), F32)],
            axis=0,
        )
        top, rest = split(node)
        result = dot(high, top) + (dot(high, rest) + dot(low, top))
        for k in range(10):
            faces_ref[k, :, part] = result[8 * k:8 * k + 3]
        copy = pltpu.make_async_copy(faces_ref.at[:, :, part], out_ref.at[:, :, part], sems.at[i])
        copy.start()
        copies.append(copy)
    for copy in copies:
        copy.wait()


VMEM = pl.BlockSpec(memory_space=pltpu.VMEM)
HBM = pl.BlockSpec(memory_space=pl.ANY)


def call(kernel, outs, scratch, *args, hbm=(), out_specs=None, limit=28, alias=None):
    single = not isinstance(outs, (list, tuple))
    shapes = [outs] if single else list(outs)
    result = pl.pallas_call(
        kernel,
        out_shape=shapes,
        in_specs=[HBM if i in hbm else VMEM for i in range(len(args))],
        out_specs=out_specs or [VMEM] * len(shapes),
        scratch_shapes=scratch,
        input_output_aliases=alias or {},
        compiler_params=pltpu.CompilerParams(vmem_limit_bytes=limit * 1024 * 1024),
    )(*args)
    return result[0] if single else result


def arr(*shape, dtype=F32):
    return jax.ShapeDtypeStruct(shape, dtype)


def ring(axis, step):
    count = lax.axis_size(axis)
    return [(i, (i + step) % count) for i in range(count)]


def shift_pair(toward_low, toward_high, axis):
    return lax.ppermute(toward_low, axis, ring(axis, -1)), lax.ppermute(toward_high, axis, ring(axis, 1))


def local(face_owner, face_element, element_state, lift, face_scale, transfer, stiffness_ref, element_scale, displacement_prev):
    owner = face_owner.reshape(1, FACES)
    element = face_element.reshape(1, FACES)
    scale = face_scale.reshape(1, FACES)
    prev = displacement_prev.reshape(12, ROWS, COLS)

    msg, rank, strip = call(
        face_kernel,
        [arr(OWNERS, 1, 896), arr(1, FACES), arr(2, STRIP, 8, COLS)],
        [
            pltpu.VMEM((1, FACES), I32), pltpu.VMEM((1, FACES), I32), pltpu.VMEM((110, FACES), BF16),
            pltpu.VMEM((1, FACES), F32), pltpu.VMEM((30, 110), BF16), pltpu.VMEM((4, 10), F32),
            pltpu.VMEM((2, 13, 8, COLS), F32),
            pltpu.VMEM((256, 2 * STEP), BF16), pltpu.VMEM((4 * OWNERS, STEP), BF16), pltpu.VMEM((4 * OWNERS, 256), F32),
            pltpu.SemaphoreType.DMA((12,)),
        ],
        owner, element, element_state, scale, lift, transfer, prev, element_scale,
        hbm=(0, 1, 2, 3, 4, 5, 6, 7), limit=LIMIT, out_specs=[VMEM, VMEM, HBM],
    )
    got = lax.all_to_all(msg, ("grp", "dev"), split_axis=0, concat_axis=0)
    mat = call(matrix_kernel, arr(192, 192, dtype=BF16), [], stiffness_ref)

    north, south, turned, mark = call(
        edge_scatter_kernel,
        [arr(PLANES, 8, COLS), arr(PLANES, 8, COLS), arr(2, 8, 128, 128), arr(64, 128)],
        [
            pltpu.VMEM((24 * 16, 2048), BF16),
            pltpu.VMEM((COLS, 2048), BF16),
            pltpu.VMEM((24 * 16, COLS), F32),
            pltpu.SemaphoreType.DMA((2,)),
        ],
        got, strip,
        hbm=(1,),
    )
    below, above = shift_pair(north, south, "grp")
    load = call(
        scatter_kernel,
        arr(12, ROWS, COLS),
        [
            pltpu.VMEM((24 * INNER, 2048), BF16),
            pltpu.VMEM((COLS, 2048), BF16),
            pltpu.VMEM((24 * INNER, COLS), F32),
        ],
        turned, mark, north, south,
    )
    west, east = call(
        columns_kernel, [arr(PAD_R, 256), arr(PAD_R, 256)], [], load, prev, element_scale, below, above
    )
    from_east, from_west = shift_pair(west, east, "dev")
    pad = call(fill_kernel, arr(PLANES, PAD_R, PAD_C), [], load, prev, element_scale, below, above)

    shell, back, _ = call(
        sweep_kernel,
        [arr(12, ROWS, COLS), arr(OWNERS, 1, 768), arr(PLANES, PAD_R, PAD_C)],
        [
            pltpu.VMEM((PAD_R // 16, 192, 2 * PAD_C), BF16),
            pltpu.VMEM((12 * HALF, 1024), BF16),
            pltpu.VMEM((8, 128, 128), F32),
        ],
        pad, from_east, from_west, mat, mark,
        alias={0: 2},
    )
    returned = lax.all_to_all(back, ("grp", "dev"), split_axis=0, concat_axis=0)
    faces = call(
        return_kernel,
        arr(10, 3, FACES),
        [
            pltpu.VMEM((384, 512), BF16),
            pltpu.VMEM((4 * OWNERS, STEP), BF16),
            pltpu.VMEM((10, 3, FACES), F32),
            pltpu.SemaphoreType.DMA((FACES // STEP,)),
        ],
        returned, owner, rank, transfer,
        out_specs=[HBM],
    )
    return shell.reshape(4, 3, ROWS, COLS), jnp.transpose(faces, (1, 0, 2))


def solution(mesh):
    placed = (
        P(("grp", "dev"), None),
        P(("grp", "dev")),
        P(None, ("grp", "dev")),
        P(),
        P(("grp", "dev")),
        P(),
        P(),
        P("grp", "dev"),
        P(None, None, "grp", "dev"),
    )
    return jax.shard_map(
        local,
        mesh=mesh,
        in_specs=placed,
        out_specs=(P(None, None, "grp", "dev"), P(None, None, ("grp", "dev"))),
        check_vma=False,
    )
```

```python
import functools

import jax
import jax.numpy as jnp
from jax import lax
from jax.experimental import pallas as pl
from jax.experimental.pallas import tpu as pltpu
from jax.sharding import PartitionSpec as P

SWEEPS = 8
WEIGHT = 2.2
HIGHEST = lax.Precision.HIGHEST
F32 = jnp.float32
BF16 = jnp.bfloat16
I32 = jnp.int32

OWNERS = 128
CAP = 64
COLS = 256
ROWS = 64
PAD_R = 80
PAD_C = 384
FACES = 4096
CHUNK = 256
STEP = 2048
HALF = 32
PLANES = 25
STRIP = 4096
LIMIT = 60
NT = (((1,), (1,)), ((), ()))


def iota(shape, dim):
    return lax.broadcasted_iota(I32, shape, dim)


def dot(a, b):
    return jnp.dot(a, b, preferred_element_type=F32)


def dot_nt(a, b):
    return lax.dot_general(a, b, NT, preferred_element_type=F32)


def exact(a, b):
    return jnp.dot(a, b, precision=HIGHEST, preferred_element_type=F32)


def one_hot(flag):
    return flag.astype(F32).astype(BF16)


def split(x):
    high = x.astype(BF16)
    return high, (x - high.astype(F32)).astype(BF16)


def hot(flag):
    return jnp.where(flag, jnp.ones((), BF16), jnp.zeros((), BF16))


def spread_row(row):
    return jnp.broadcast_to(row, (16, row.shape[1])).astype(BF16)


def hot_rows(row, count):
    wide = spread_row(row)
    step = iota((16, row.shape[1]), 0).astype(F32).astype(BF16)
    return [hot(step == wide - 16.0 * k) for k in range(count // 16)]


def quarters(owner, quarter):
    pieces = hot_rows(owner, OWNERS)
    wide = spread_row(quarter)
    for q in range(4):
        here = hot(wide == q)
        for k, piece in enumerate(pieces):
            yield q * OWNERS + 16 * k, piece * here


def face_kernel(owner_hbm, elem_hbm, state_hbm, scale_hbm, lift_hbm, transfer_hbm, prev_hbm, shell_hbm,
                msg_ref, rank_ref, strip_ref,
                owner_ref, elem_ref, state_ref, scale_ref, lift_ref, transfer_ref, stage_ref, x_ref, hot_ref, acc_ref,
                sems):
    copies = [
        pltpu.make_async_copy(src, dst, sems.at[i])
        for i, (src, dst) in enumerate((
            (owner_hbm, owner_ref), (transfer_hbm, transfer_ref), (lift_hbm, lift_ref),
            (elem_hbm, elem_ref), (scale_hbm, scale_ref), (state_hbm, state_ref),
            (prev_hbm.at[:, 0:8, :], stage_ref.at[0, 0:12]),
            (prev_hbm.at[:, ROWS - 8:ROWS, :], stage_ref.at[1, 0:12]),
            (shell_hbm.at[0:8, :], stage_ref.at[0, 12]),
            (shell_hbm.at[ROWS - 8:ROWS, :], stage_ref.at[1, 12]),
        ))
    ]
    for copy in copies:
        copy.start()
    x_ref[...] = jnp.zeros_like(x_ref)
    acc_ref[...] = jnp.zeros_like(acc_ref)
    before = iota((CHUNK, 2 * CHUNK), 0)
    upper = iota((CHUNK, 2 * CHUNK), 1)
    upper = one_hot((before < upper) | (upper >= CHUNK))
    copies[0].wait()

    def ranks(i, base):
        part = pl.ds(pl.multiple_of(i * CHUNK, CHUNK), CHUNK)
        mine = (iota((OWNERS, CHUNK), 0) == owner_ref[:, part]).astype(F32)
        counts = dot(mine.astype(BF16), upper)
        rank_ref[:, part] = jnp.sum(mine * (counts[:, :CHUNK] + base), axis=0, keepdims=True)
        return base + counts[:, CHUNK:]

    lax.fori_loop(0, FACES // CHUNK, ranks, jnp.zeros((OWNERS, CHUNK), F32), unroll=True)
    for copy in copies[1:]:
        copy.wait()
    keeps = [pltpu.make_async_copy(stage_ref.at[i], strip_ref.at[i, 0:13], sems.at[10 + i]) for i in range(2)]
    for copy in keeps:
        copy.start()
    spread = jnp.concatenate(
        [jnp.pad(transfer_ref[...], ((0, 0), (10 * c, 20 - 10 * c))) for c in range(3)], axis=0
    )
    weights = exact(spread, lift_ref[...].astype(F32))
    high, low = split(weights)

    def body(i, carry):
        part = pl.ds(pl.multiple_of(i * STEP, STEP), STEP)
        rank = rank_ref[:, part].astype(I32)
        for at, piece in quarters(owner_ref[:, part].astype(F32), (rank >> 4).astype(F32)):
            hot_ref[at:at + 16, :] = piece
        place, = hot_rows((rank & 15).astype(F32), 16)
        state = state_ref[:, part]
        load = (dot(high, state) + dot(low, state)) * scale_ref[:, part]
        marker = (elem_ref[:, part] + 1).astype(F32)
        for c in range(13):
            at = 4 * (c % 3) + c // 3
            row = load[at:at + 1] if c < 12 else marker
            top, rest = split(jnp.broadcast_to(row, (16, STEP)))
            x_ref[16 * c:16 * c + 16, :STEP] = place * top
            x_ref[16 * c:16 * c + 16, STEP:] = place * rest
        acc_ref[...] += dot_nt(hot_ref[...], x_ref[:, :STEP]) + dot_nt(hot_ref[...], x_ref[:, STEP:])
        return carry

    lax.fori_loop(0, FACES // STEP, body, 0)
    lane = iota((OWNERS, 128), 1)
    marks = jnp.zeros((OWNERS, 128), F32)
    last = None
    for q in range(4):
        mine = slice(q * OWNERS, (q + 1) * OWNERS)
        msg_ref[:, 0, 128 * q:128 * q + 128] = acc_ref[mine, 0:128]
        late = acc_ref[mine, 128:256]
        marks = jnp.where(lane // 16 == q, pltpu.roll(late, 64 + 16 * q, 1), marks)
        if q % 2:
            at = 512 + 128 * (q // 2)
            msg_ref[:, 0, at:at + 128] = jnp.where(lane < 64, last, pltpu.roll(late, 64, 1))
        last = late
    msg_ref[:, 0, 768:896] = marks
    for copy in keeps:
        copy.wait()


def places(marker):
    element = marker.astype(I32) - 1
    row, col = element >> 8, (element & 255).astype(F32)
    pieces = hot_rows(col, COLS)
    wide = spread_row(row.astype(F32))
    low, high = hot(wide < HALF), hot(wide >= HALF)
    columns = [piece * low for piece in pieces] + [piece * high for piece in pieces]
    return (row & (HALF - 1)).astype(F32), columns


def build(turned_ref, mark_ref, q, count, number, a_ref, col_ref):
    for h in range(2):
        markers = mark_ref[pl.ds(pl.multiple_of(16 * q + 8 * h, 8), 8), :]
        for k in range(8):
            lanes = slice(1024 * h + 128 * k, 1024 * h + 128 * k + 128)
            element = markers[k:k + 1].astype(I32) - 1
            for b, piece in enumerate(hot_rows((element & 255).astype(F32), COLS)):
                col_ref[16 * b:16 * b + 16, lanes] = piece
            row_hot = hot_rows(number(element >> 8).astype(F32), count)
            for part in range(2):
                for c in range(12):
                    first = 16 * (c % 8) + 8 * h
                    values = turned_ref[part, 2 * q + c // 8, first:first + 8, :]
                    value = spread_row(values[k:k + 1])
                    at = (12 * part + c) * count
                    for b, piece in enumerate(row_hot):
                        a_ref[at + 16 * b:at + 16 * b + 16, lanes] = piece * value


def edge_scatter_kernel(msg_ref, strip_ref, north_ref, south_ref, turned_ref, mark_ref,
                        a_ref, col_ref, acc_ref, sems):
    copies = [
        pltpu.make_async_copy(strip_ref.at[i, 0:13], ref.at[12:PLANES], sems.at[i])
        for i, ref in enumerate((north_ref, south_ref))
    ]
    for copy in copies:
        copy.start()
    acc_ref[...] = jnp.zeros_like(acc_ref)
    mark_ref[...] = jnp.transpose(msg_ref[:, 0, 768:896])[:64]
    for j in range(6):
        turned = jnp.transpose(msg_ref[:, 0, 128 * j:128 * j + 128]) * (1.0 / WEIGHT)
        top = turned.astype(BF16).astype(F32)
        for part, value in enumerate((top, turned - top)):
            if j < 4:
                turned_ref[part, 2 * j] = value
            else:
                turned_ref[part, 4 * j - 15, 0:64] = value[0:64]
                turned_ref[part, 4 * j - 13, 0:64] = value[64:128]

    def body(q, carry):
        build(
            turned_ref, mark_ref, q, 16,
            lambda row: jnp.where(row < 8, row, jnp.where(row >= ROWS - 8, row - (ROWS - 16), -1)), a_ref, col_ref,
        )
        acc_ref[...] += dot_nt(a_ref[...], col_ref[...])
        return carry

    lax.fori_loop(0, 4, body, 0)
    for c in range(12):
        strip = acc_ref[16 * c:16 * c + 16] + acc_ref[192 + 16 * c:208 + 16 * c]
        north_ref[c] = strip[0:8]
        south_ref[c] = strip[8:16]
    for copy in copies:
        copy.wait()


INNER = ROWS - 16


def scatter_kernel(turned_ref, mark_ref, north_ref, south_ref, load_ref, a_ref, col_ref, acc_ref):
    acc_ref[...] = jnp.zeros_like(acc_ref)

    def body(q, carry):
        build(turned_ref, mark_ref, q, INNER, lambda row: row - 8, a_ref, col_ref)
        acc_ref[...] += dot_nt(a_ref[...], col_ref[...])
        return carry

    lax.fori_loop(0, 4, body, 0)
    for c in range(12):
        load_ref[c, 0:8, :] = north_ref[c]
        load_ref[c, 8:8 + INNER, :] = acc_ref[INNER * c:INNER * c + INNER] + acc_ref[INNER * (12 + c):INNER * (13 + c)]
        load_ref[c, ROWS - 8:ROWS, :] = south_ref[c]


def matrix_kernel(stiff_ref, mat_ref):
    eye = (iota((12, 12), 0) == iota((12, 12), 1)).astype(F32)
    approx = eye / 5.0
    rest = eye - exact(stiff_ref[...], approx)
    for turn in range(8):
        approx = approx + exact(approx, rest)
        if turn < 7:
            rest = exact(rest, rest)
    tall = (iota((96, 12), 0) // 8 == iota((96, 12), 1)).astype(F32)
    wide = (iota((12, 96), 1) // 8 == iota((12, 96), 0)).astype(F32)
    big = exact(exact(tall, approx * WEIGHT), wide)
    big = jnp.where(iota((96, 96), 0) % 8 == iota((96, 96), 1) % 8, big, 0.0)
    high, low = split(big)
    mat_ref[0:96, :] = jnp.concatenate([high, high], axis=1)
    mat_ref[96:192, :] = jnp.concatenate([low, jnp.zeros_like(low)], axis=1)


def columns_kernel(load_ref, prev_ref, scale_ref, south_ref, north_ref, west_ref, east_ref):
    for at, rows, pick in (
        (0, ROWS, lambda p, lanes: scale_ref[:, lanes] if p == 24 else load_ref[p, :, lanes] if p < 12 else prev_ref[p - 12, :, lanes]),
        (ROWS, 8, lambda p, lanes: south_ref[p, :, lanes]),
        (ROWS + 8, 8, lambda p, lanes: north_ref[p, :, lanes]),
    ):
        group = iota((rows, 128), 1) // 8
        for tile in range(2):
            west = jnp.zeros((rows, 128), F32)
            east = jnp.zeros((rows, 128), F32)
            for p in range(16 * tile, min(PLANES, 16 * tile + 16)):
                i = p % 16
                low = pick(p, slice(0, 128))
                high = pick(p, slice(128, 256))
                west = jnp.where(group == i, pltpu.roll(low, 8 * i, 1) if i else low, west)
                east = jnp.where(group == i, pltpu.roll(high, (8 * i + 8) % 128, 1), east)
            west_ref[at:at + rows, 128 * tile:128 * tile + 128] = west
            east_ref[at:at + rows, 128 * tile:128 * tile + 128] = east


def row_ok(shape):
    grp = lax.axis_index("grp")
    row = iota(shape, 0)
    return (row < ROWS) | ((row < ROWS + 8) & (grp < lax.axis_size("grp") - 1)) | ((row >= ROWS + 8) & (grp > 0))


def settle(pad_ref, lanes, ok):
    pad_ref[24, :, lanes] = jnp.where(ok, 1.0 / jnp.where(ok, pad_ref[24, :, lanes], 1.0), 0.0)
    for c in range(12):
        pad_ref[12 + c, :, lanes] = jnp.where(ok, pad_ref[12 + c, :, lanes], 0.0)


def fill_kernel(load_ref, prev_ref, scale_ref, south_ref, north_ref, pad_ref):
    for p in range(PLANES):
        pad_ref[p, 0:ROWS, 0:COLS] = scale_ref[...] if p == 24 else load_ref[p] if p < 12 else prev_ref[p - 12]
        pad_ref[p, ROWS:ROWS + 8, 0:COLS] = south_ref[p]
        pad_ref[p, ROWS + 8:PAD_R, 0:COLS] = north_ref[p]
        pad_ref[p, :, COLS:PAD_C] = jnp.zeros((PAD_R, PAD_C - COLS), F32)
    settle(pad_ref, slice(0, COLS), row_ok((PAD_R, COLS)))


def sweep_kernel(pad_in, from_east_ref, from_west_ref, mat_ref, mark_ref,
                 out_ref, ret_ref, pad_ref, x_ref, hl_ref, turned_ref):
    del pad_in
    lane = iota((PAD_R, 128), 1)
    for p in range(PLANES):
        tile = slice(128 * (p // 16), 128 * (p // 16) + 128)
        low = pltpu.roll(from_east_ref[:, tile], (128 - 8 * (p % 16)) % 128, 1)
        high = pltpu.roll(from_west_ref[:, tile], (248 - 8 * (p % 16)) % 128, 1)
        pad_ref[p, :, COLS:PAD_C] = jnp.where(lane < 8, low, jnp.where(lane >= 120, high, 0.0))
    dev = lax.axis_index("dev")
    ok = row_ok((PAD_R, 128)) & (
        ((lane < 8) & (dev < lax.axis_size("dev") - 1)) | ((lane >= 120) & (dev > 0))
    )
    settle(pad_ref, slice(COLS, PAD_C), ok)
    along = ((1, 1), (0, PAD_C - 1), (3, 1), (2, PAD_C - 1))
    across = ((2, 1), (3, 1), (0, PAD_R - 1), (1, PAD_R - 1))

    def right_side(at):
        n, c = divmod(at, 3)
        return (
            pad_ref[at]
            + pltpu.roll(pad_ref[12 + 3 * along[n][0] + c], along[n][1], 1)
            + pltpu.roll(pad_ref[12 + 3 * across[n][0] + c], across[n][1], 0)
        )

    def sweep(turn, carry):
        for at in range(0, 12, 2):
            first, second = right_side(at), right_side(at + 1)
            for b in range(PAD_R // 8):
                rows = slice(8 * b, 8 * b + 8)
                top, rest = split(jnp.concatenate([first[rows], second[rows]], axis=0))
                lanes = slice(PAD_C * (b % 2), PAD_C * (b % 2) + PAD_C)
                x_ref[b // 2, 8 * at:8 * at + 16, lanes] = top
                x_ref[b // 2, 96 + 8 * at:96 + 8 * at + 16, lanes] = rest
        for b in range(PAD_R // 16):
            solved = dot(mat_ref[...], x_ref[b])
            for h in range(2):
                rows = slice(16 * b + 8 * h, 16 * b + 8 * h + 8)
                lanes = slice(PAD_C * h, PAD_C * h + PAD_C)
                factor = pad_ref[24, rows]
                for at in range(12):
                    pad_ref[12 + at, rows] = (
                        solved[8 * at:8 * at + 8, lanes] + solved[96 + 8 * at:96 + 8 * at + 8, lanes]
                    ) * factor
        return carry

    lax.fori_loop(0, SWEEPS, sweep, 0, unroll=8)
    for c in range(12):
        value = pad_ref[12 + c, 0:ROWS, 0:COLS]
        out_ref[c] = value
        top, rest = split(value)
        for b in range(2):
            part = slice(HALF * b, HALF * (b + 1))
            hl_ref[c * HALF:(c + 1) * HALF, COLS * b:COLS * (b + 1)] = top[part]
            hl_ref[c * HALF:(c + 1) * HALF, 512 + COLS * b:512 + COLS * (b + 1)] = rest[part]

    def gather(q, carry):
        markers = mark_ref[pl.ds(pl.multiple_of(16 * q, 16), 16), :]
        row, columns = places(jnp.concatenate([markers[k:k + 1] for k in range(16)], axis=1))
        columns = jnp.concatenate(columns, axis=0)
        found = dot(hl_ref[:, :512], columns) + dot(hl_ref[:, 512:], columns)
        here = iota((HALF, 2048), 0).astype(F32) == row
        for c in range(12):
            value = jnp.sum(jnp.where(here, found[c * HALF:(c + 1) * HALF], 0.0), axis=0, keepdims=True)
            value = jnp.concatenate([value[:, 128 * k:128 * k + 128] for k in range(16)], axis=0)
            turned_ref[2 * q + c // 8, 16 * (c % 8):16 * (c % 8) + 16, :] = value
        return carry

    lax.fori_loop(0, 4, gather, 0, unroll=2)
    for q in range(4):
        ret_ref[:, 0, 128 * q:128 * q + 128] = jnp.transpose(turned_ref[2 * q])
    for j in range(2):
        late = jnp.concatenate([turned_ref[4 * j + 1, 0:64], turned_ref[4 * j + 3, 0:64]], axis=0)
        ret_ref[:, 0, 512 + 128 * j:640 + 128 * j] = jnp.transpose(late)


def return_kernel(ret_ref, owner_ref, rank_ref, transfer_ref, out_ref, l_ref, hot_ref, faces_ref, sems):
    for j in range(6):
        top, rest = split(jnp.transpose(ret_ref[:, 0, 128 * j:128 * j + 128]))
        for part, value in enumerate((top, rest)):
            at = 192 * part
            if j < 4:
                l_ref[at:at + 128, 128 * j:128 * j + 128] = value
            else:
                lane = 256 * (j - 4)
                l_ref[at + 128:at + 192, lane:lane + 128] = value[0:64]
                l_ref[at + 128:at + 192, lane + 128:lane + 256] = value[64:128]
    pick = (iota((80, 10), 0) // 8 == iota((80, 10), 1)).astype(F32)
    spread = lax.dot_general(pick, transfer_ref[...], NT, precision=HIGHEST, preferred_element_type=F32)
    spread = exact(spread, (iota((4, 16), 1) // 3 == iota((4, 16), 0)).astype(F32))
    spread = jnp.where(iota((80, 16), 0) % 8 == iota((80, 16), 1) % 3, spread, 0.0)
    high, low = split(spread)
    copies = []
    for i in range(FACES // STEP):
        part = slice(i * STEP, (i + 1) * STEP)
        rank = rank_ref[:, part].astype(I32)
        for at, piece in quarters(owner_ref[:, part].astype(F32), (rank >> 4).astype(F32)):
            hot_ref[at:at + 16, :] = piece
        found = dot(l_ref[...], hot_ref[...])
        found = found[:192] + found[192:]
        here = iota((16, STEP), 0) == (rank & 15)
        node = jnp.concatenate(
            [jnp.sum(jnp.where(here, found[16 * c:16 * c + 16], 0.0), axis=0, keepdims=True) for c in range(12)]
            + [jnp.zeros((4, STEP), F32)],
            axis=0,
        )
        top, rest = split(node)
        result = dot(high, top) + (dot(high, rest) + dot(low, top))
        for k in range(10):
            faces_ref[k, :, part] = result[8 * k:8 * k + 3]
        copy = pltpu.make_async_copy(faces_ref.at[:, :, part], out_ref.at[:, :, part], sems.at[i])
        copy.start()
        copies.append(copy)
    for copy in copies:
        copy.wait()


VMEM = pl.BlockSpec(memory_space=pltpu.VMEM)
HBM = pl.BlockSpec(memory_space=pl.ANY)


def call(kernel, outs, scratch, *args, hbm=(), out_specs=None, limit=28, alias=None):
    single = not isinstance(outs, (list, tuple))
    shapes = [outs] if single else list(outs)
    result = pl.pallas_call(
        kernel,
        out_shape=shapes,
        in_specs=[HBM if i in hbm else VMEM for i in range(len(args))],
        out_specs=out_specs or [VMEM] * len(shapes),
        scratch_shapes=scratch,
        input_output_aliases=alias or {},
        compiler_params=pltpu.CompilerParams(vmem_limit_bytes=limit * 1024 * 1024),
    )(*args)
    return result[0] if single else result


def arr(*shape, dtype=F32):
    return jax.ShapeDtypeStruct(shape, dtype)


def ring(axis, step):
    count = lax.axis_size(axis)
    return [(i, (i + step) % count) for i in range(count)]


def shift_pair(toward_low, toward_high, axis):
    return lax.ppermute(toward_low, axis, ring(axis, -1)), lax.ppermute(toward_high, axis, ring(axis, 1))


def local(face_owner, face_element, element_state, lift, face_scale, transfer, stiffness_ref, element_scale, displacement_prev):
    owner = face_owner.reshape(1, FACES)
    element = face_element.reshape(1, FACES)
    scale = face_scale.reshape(1, FACES)
    prev = displacement_prev.reshape(12, ROWS, COLS)

    msg, rank, strip = call(
        face_kernel,
        [arr(OWNERS, 1, 896), arr(1, FACES), arr(2, STRIP, 8, COLS)],
        [
            pltpu.VMEM((1, FACES), I32), pltpu.VMEM((1, FACES), I32), pltpu.VMEM((110, FACES), BF16),
            pltpu.VMEM((1, FACES), F32), pltpu.VMEM((30, 110), BF16), pltpu.VMEM((4, 10), F32),
            pltpu.VMEM((2, 13, 8, COLS), F32),
            pltpu.VMEM((256, 2 * STEP), BF16), pltpu.VMEM((4 * OWNERS, STEP), BF16), pltpu.VMEM((4 * OWNERS, 256), F32),
            pltpu.SemaphoreType.DMA((12,)),
        ],
        owner, element, element_state, scale, lift, transfer, prev, element_scale,
        hbm=(0, 1, 2, 3, 4, 5, 6, 7), limit=LIMIT, out_specs=[VMEM, VMEM, HBM],
    )
    got = lax.all_to_all(msg, ("grp", "dev"), split_axis=0, concat_axis=0)
    mat = call(matrix_kernel, arr(192, 192, dtype=BF16), [], stiffness_ref)

    north, south, turned, mark = call(
        edge_scatter_kernel,
        [arr(PLANES, 8, COLS), arr(PLANES, 8, COLS), arr(2, 8, 128, 128), arr(64, 128)],
        [
            pltpu.VMEM((24 * 16, 2048), BF16),
            pltpu.VMEM((COLS, 2048), BF16),
            pltpu.VMEM((24 * 16, COLS), F32),
            pltpu.SemaphoreType.DMA((2,)),
        ],
        got, strip,
        hbm=(1,),
    )
    below, above = shift_pair(north, south, "grp")
    load = call(
        scatter_kernel,
        arr(12, ROWS, COLS),
        [
            pltpu.VMEM((24 * INNER, 2048), BF16),
            pltpu.VMEM((COLS, 2048), BF16),
            pltpu.VMEM((24 * INNER, COLS), F32),
        ],
        turned, mark, north, south,
    )
    west, east = call(
        columns_kernel, [arr(PAD_R, 256), arr(PAD_R, 256)], [], load, prev, element_scale, below, above
    )
    from_east, from_west = shift_pair(west, east, "dev")
    pad = call(fill_kernel, arr(PLANES, PAD_R, PAD_C), [], load, prev, element_scale, below, above)

    shell, back, _ = call(
        sweep_kernel,
        [arr(12, ROWS, COLS), arr(OWNERS, 1, 768), arr(PLANES, PAD_R, PAD_C)],
        [
            pltpu.VMEM((PAD_R // 16, 192, 2 * PAD_C), BF16),
            pltpu.VMEM((12 * HALF, 1024), BF16),
            pltpu.VMEM((8, 128, 128), F32),
        ],
        pad, from_east, from_west, mat, mark,
        alias={0: 2},
    )
    returned = lax.all_to_all(back, ("grp", "dev"), split_axis=0, concat_axis=0)
    faces = call(
        return_kernel,
        arr(10, 3, FACES),
        [
            pltpu.VMEM((384, 512), BF16),
            pltpu.VMEM((4 * OWNERS, STEP), BF16),
            pltpu.VMEM((10, 3, FACES), F32),
            pltpu.SemaphoreType.DMA((FACES // STEP,)),
        ],
        returned, owner, rank, transfer,
        out_specs=[HBM],
    )
    return shell.reshape(4, 3, ROWS, COLS), jnp.transpose(faces, (1, 0, 2))


def solution(mesh):
    placed = (
        P(("grp", "dev"), None),
        P(("grp", "dev")),
        P(None, ("grp", "dev")),
        P(),
        P(("grp", "dev")),
        P(),
        P(),
        P("grp", "dev"),
        P(None, None, "grp", "dev"),
    )
    return jax.shard_map(
        local,
        mesh=mesh,
        in_specs=placed,
        out_specs=(P(None, None, "grp", "dev"), P(None, None, ("grp", "dev"))),
        check_vma=False,
    )
```
